128 devices in a mesh: span: 16 (over x_lo, y, core), patch: 8 (over x_hi, z).
Axes of the slice: x: 4 (x_hi: 2, x_lo: 2; x = x_hi * 2 + x_lo), y: 4, z: 4, core: 2. Of those that a mesh axis runs over, the one named last changes fastest.
Arguments:
- queries: bfloat16 [16, 512, 3072], P('span', 'patch'), may hold values from -8 to 8
- keys: bfloat16 [16, 512, 3072], P('span', 'patch'), may hold values from -8 to 8
- values: bfloat16 [16, 512, 3072], P('span', 'patch'), may hold values from -6 to 6
- q_gain: float32 [3072], replicated, may hold values from 0.1 to 1.9
- k_gain: float32 [3072], replicated, may hold values from 0.1 to 1.9
- gate_table: float32 [50, 3072], replicated, may hold values from 0.3 to 1.7
- noise_step: int32 [16], P('span'), may hold values from 0 to 49
- block_mask: int32 [16, 16], replicated, may hold values from 0 to 1, as said below
- finished: int32 [1], replicated, may hold values from 0 to 15
Outputs:
- mixed: bfloat16 [16, 512, 3072], P('span', 'patch')
- committed_k: bfloat16 [512, 3072], P('span', 'patch')
- committed_v: bfloat16 [512, 3072], P('span', 'patch')
The draws below stay inside these ranges and needn't reach their ends.
Inputs may be any that keep to these rules, and one draw needn't show every extreme that they name: block-causal with a history window: for each span c there is a first span s[c] <= c, and block_mask[c, j] = 1 exactly for s[c] <= j <= c.
All inputs are finite; a program needn't handle non-finite values.
Results may differ from the reference program's by a relative error of at most 0.0085.
Values may be sent and summed in bfloat16 or wider, within the bound.
No kernel may reach another device: no remote copies, remote signals or barrier semaphores. Data moves between devices by JAX's collectives and lax.ppermute only.
A program may use at most 128 MiB of HBM per device.

```python
import jax
import jax.numpy as jnp
from jax import lax

HEADS = 24
HEAD_DIM = 128
STEPS = 50
HD = 3072
SPANS = 16
PTOK = 512


def shaped_rows(key):
    shape = (SPANS, PTOK, HEADS * HEAD_DIM)
    return jnp.clip(jax.random.normal(key, shape, jnp.float32), -6.0, 6.0)


def lax_iota(shape, dim):
    return jax.lax.broadcasted_iota(jnp.int32, shape, dim)


def draw_queries(key, part):
    key = jax.random.fold_in(key, 3)
    return shaped_rows(key).astype(jnp.bfloat16)


def draw_keys(key, part):
    key = jax.random.fold_in(key, 4)
    return shaped_rows(key).astype(jnp.bfloat16)


def draw_block_mask(key, part):
    key = jax.random.fold_in(key, 5)
    rows_only = jnp.arange(SPANS, dtype=jnp.int32)
    first = jax.random.randint(key, (SPANS,), 0, rows_only + 1)
    row = lax_iota((SPANS, SPANS), 0)
    column = lax_iota((SPANS, SPANS), 1)
    inside = (column <= row) & (column >= first[:, None])
    return jnp.where(inside, 1, 0).astype(jnp.int32)


def plant(drawn, own_key, low, top_value):
    place = [jax.random.randint(jax.random.fold_in(own_key, axis), (), 0, length) for axis, length in enumerate(drawn.shape)]
    main_axis = drawn.shape.index(max(drawn.shape))
    next_to = place[:main_axis] + [(place[main_axis] + 1) % drawn.shape[main_axis]] + place[main_axis + 1:]
    return drawn.at[tuple(place)].set(low).at[tuple(next_to)].set(top_value)


def shard_levels(stream_key, extent, pieces, low, high):
    level, own = 1.0, jax.random.fold_in(stream_key, 6)
    for axis_at, shards_of in pieces:
        draws = jnp.exp(jax.random.uniform(jax.random.fold_in(own, axis_at), (shards_of,), jnp.float32, low / len(pieces), high / len(pieces)))
        level = level * jnp.repeat(draws, extent[axis_at] // shards_of).reshape([-1 if axis == axis_at else 1 for axis in range(len(extent))])
    return level


def noise(rng, dims, width, reach, cuts=(), kind=jnp.bfloat16):
    entries = jax.random.normal(rng, dims, jnp.float32) * width
    if len(cuts) > 0:
        entries = shard_levels(rng, dims, cuts, -0.22, 0.18) * entries
    return jnp.clip(entries, min=-reach, max=reach).astype(kind)


def setup_inputs(seed: int = 0) -> dict:
    splits = jax.random.split(jax.random.key(seed), 10)
    return {
        "queries": draw_queries(jax.random.fold_in(splits[9], 71), 0),
        "keys": draw_keys(jax.random.fold_in(splits[9], 71), 0),
        "values": noise(splits[2], (SPANS, PTOK, HD), 1.0, 6.0, ((0, 16), (1, 8))),
        "q_gain": jnp.clip(1.0 + 0.18 * jax.random.normal(splits[3], (HD,), jnp.float32), 0.1, 1.9),
        "k_gain": jnp.clip(1.0 + 0.18 * jax.random.normal(splits[4], (HD,), jnp.float32), 0.1, 1.9),
        "gate_table": jnp.clip(jax.random.uniform(splits[5], (STEPS, HD), jnp.float32, 0.3, 1.7), 0.3, 1.7),
        "noise_step": plant(jax.random.randint(splits[6], (SPANS,), 0, STEPS), jax.random.fold_in(splits[6], 1), 0, STEPS - 1).astype(jnp.int32),
        "block_mask": draw_block_mask(jax.random.fold_in(splits[9], 71), 0),
        "finished": jax.random.randint(splits[8], (1,), 0, SPANS).astype(jnp.int32),
    }


def normalize(rows, gain):
    wide = rows.astype(jnp.float32)
    factor = lax.rsqrt(lax.optimization_barrier(jnp.mean(wide * wide, axis=-1, keepdims=True)) + 1e-06)
    return (wide * factor * gain).astype(jnp.bfloat16)

def one_head(query_h, key_h, value_h, allowed):
    scores = jnp.dot(query_h, key_h.T, preferred_element_type=jnp.float32) * HEAD_DIM ** (-0.5)
    scores = jnp.where(allowed[None, :], scores, -jnp.inf)
    largest = lax.optimization_barrier(jnp.max(scores, axis=1, keepdims=True))
    weight = jnp.exp(scores - largest)
    total = lax.optimization_barrier(jnp.sum(weight, axis=1, keepdims=True))
    summed = jnp.dot(weight.astype(jnp.bfloat16), value_h, preferred_element_type=jnp.float32)
    return (summed / total).astype(jnp.bfloat16)

def reference(queries, keys, values, q_gain, k_gain, gate_table, noise_step, block_mask, finished):
    qn = normalize(queries, q_gain)
    kn = normalize(keys, k_gain)
    key_heads = kn.reshape(SPANS * PTOK, HEADS, HEAD_DIM).transpose(1, 0, 2)
    value_heads = values.reshape(SPANS * PTOK, HEADS, HEAD_DIM).transpose(1, 0, 2)

    def one_span(item):
        query_c, mask_row = item
        allowed = jnp.repeat(mask_row, PTOK) > 0
        query_heads = query_c.reshape(PTOK, HEADS, HEAD_DIM).transpose(1, 0, 2)
        outs = lax.map(lambda group: one_head(group[0], group[1], group[2], allowed), (query_heads, key_heads, value_heads))
        return outs.transpose(1, 0, 2).reshape(PTOK, HD)
    attn = lax.map(one_span, (qn, block_mask))
    gates = gate_table[noise_step]
    mixed = (attn.astype(jnp.float32) * gates[:, None, :]).astype(jnp.bfloat16)
    chosen = finished[0]
    committed_k = lax.dynamic_index_in_dim(kn, chosen, 0, keepdims=False)
    committed_v = lax.dynamic_index_in_dim(values, chosen, 0, keepdims=False)
    return (mixed, committed_k, committed_v)
```

```python
import functools

import jax
import jax.numpy as jnp
from jax import lax
from jax.experimental import pallas as pl
from jax.experimental.pallas import tpu as pltpu
from jax.sharding import Mesh
from jax.sharding import PartitionSpec as P

D = 128
HEADS = 24
HD = HEADS * D
SPANS = 16
TOK = 64
HALF = TOK // 2
SLOTS = 32
CHIPS = 2 * SLOTS
ROWS = 2 * TOK + HALF
OUT_ROWS = 2 * HALF
PLANE = ("xl", "y", "xh", "z")
EPS = 1e-06
SCALE = D ** (-0.5)
VMEM = pl.BlockSpec(memory_space=pltpu.VMEM)
SMEM = pl.BlockSpec(memory_space=pltpu.SMEM)


def head_slot():
    return lax.axis_index("y") * 8 + patch_index()


def patch_index():
    return lax.axis_index("xh") * 4 + lax.axis_index("z")


def pack_kernel(q_ref, k_ref, v_ref, q_gain, k_gain, out_ref):
    def factor(ref):
        wide = ref[0].astype(jnp.float32)
        return lax.rsqrt(jnp.mean(wide * wide, axis=-1, keepdims=True) + EPS)

    q_factor = factor(q_ref)
    k_factor = factor(k_ref)
    for h in range(HEADS):
        cols = slice(h * D, (h + 1) * D)
        qn = (q_ref[0, :, cols].astype(jnp.float32) * q_factor * q_gain[:, cols]).astype(jnp.bfloat16)
        kn = (k_ref[0, :, cols].astype(jnp.float32) * k_factor * k_gain[:, cols]).astype(jnp.bfloat16)
        for x in range(2):
            out_ref[x * SLOTS + h, 0:TOK, :] = kn
            out_ref[x * SLOTS + h, TOK : 2 * TOK, :] = v_ref[0, :, cols]
            out_ref[x * SLOTS + h, 2 * TOK : ROWS, :] = qn[x * HALF : (x + 1) * HALF]


def attend_kernel(mask_ref, fin_ref, own_ref, peer_ref, out_ref):
    core = lax.axis_index("core")
    xl = lax.axis_index("xl")
    head = head_slot()

    def block(q, ref, u, state):
        most, total, summed = state
        k = ref[pl.ds(u * 8, 8), 0:TOK, :].reshape(8 * TOK, D)
        v = ref[pl.ds(u * 8, 8), TOK : 2 * TOK, :].reshape(8 * TOK, D)
        scores = lax.dot_general(q, k, (((1,), (1,)), ((), ())), preferred_element_type=jnp.float32) * SCALE
        newest = jnp.maximum(most, jnp.max(scores, axis=1, keepdims=True))
        weight = jnp.exp(scores - newest)
        factor = jnp.exp(most - newest)
        part = weight[:, 0:D]
        for i in range(1, 4):
            part = part + weight[:, i * D : (i + 1) * D]
        total = total * factor + part
        added = jnp.dot(weight.astype(jnp.bfloat16), v, preferred_element_type=jnp.float32)
        return newest, total, summed * factor + added

    @pl.when(head < HEADS)
    def _():
        def span(t, carry):
            c = 2 * t + core
            counted = mask_ref[c, 0]
            for j in range(1, SPANS):
                counted = counted + mask_ref[c, j]
            first = c + 1 - counted
            q = own_ref[pl.ds(t * 8, 8), 2 * TOK : ROWS, :].reshape(8 * HALF, D)
            state = (
                jnp.full((8 * HALF, 1), -1e30, jnp.float32),
                jnp.zeros((8 * HALF, D), jnp.float32),
                jnp.zeros((8 * HALF, D), jnp.float32),
            )
            state = lax.fori_loop(
                (first - core + 1) // 2, t + 1, lambda u, s: block(q, own_ref, u, s), state
            )
            state = lax.fori_loop(
                (first + core) // 2, t + core, lambda u, s: block(q, peer_ref, u, s), state
            )
            _, total, summed = state
            attn = summed / jnp.sum(total, axis=1, keepdims=True)
            out_ref[pl.ds(t * 8, 8), 0:HALF, :] = attn.astype(jnp.bfloat16).reshape(8, HALF, D)
            return carry

        lax.fori_loop(0, 8, span, 0)

        fin = fin_ref[0]
        column = head // 3
        start = core * HALF + xl * (HALF // 2)

        def commit(ref):
            for t in range(8):
                slot = (fin // 2) * 8 + t
                for i in range(2):
                    rows = ref[slot, pl.ds(pl.multiple_of(start + i * TOK, 16), HALF // 2), :]
                    out_ref[t * 8 + column, pl.ds(HALF + i * (HALF // 2), HALF // 2), :] = rows

        pl.when(fin % 2 == core)(lambda: commit(own_ref))
        pl.when(fin % 2 != core)(lambda: commit(peer_ref))


def finish_kernel(step_ref, in_ref, gate_ref, mixed_ref, k_ref, v_ref):
    gate = gate_ref[pl.ds(step_ref[0], 1), :]
    for h in range(HEADS):
        cols = slice(h * D, (h + 1) * D)
        for x in range(2):
            rows = slice(x * HALF, (x + 1) * HALF)
            attn = in_ref[x * SLOTS + h, 0:HALF, :].astype(jnp.float32)
            mixed_ref[0, rows, cols] = (attn * gate[:, cols]).astype(jnp.bfloat16)
    patch = patch_index()
    for i in range(3):
        for x in range(2):
            src = x * SLOTS + 3 * patch + i
            rows = slice(x * (HALF // 2), (x + 1) * (HALF // 2))
            k_ref[rows, i * D : (i + 1) * D] = in_ref[src, HALF : HALF + HALF // 2, :]
            v_ref[rows, i * D : (i + 1) * D] = in_ref[src, HALF + HALF // 2 : OUT_ROWS, :]


PARAMS = pltpu.CompilerParams(vmem_limit_bytes=40 * 1024 * 1024)


def on_device(queries, keys, values, q_gain, k_gain, gate_table, noise_step, block_mask, finished):
    bf16 = jnp.bfloat16
    packed = pl.pallas_call(
        pack_kernel,
        out_shape=jax.ShapeDtypeStruct((CHIPS, ROWS, D), bf16),
        in_specs=[VMEM] * 5,
        out_specs=VMEM,
        compiler_params=PARAMS,
    )(queries, keys, values, q_gain.reshape(1, HD), k_gain.reshape(1, HD))
    own = lax.all_to_all(packed, PLANE, 0, 0, tiled=True)
    peer = lax.ppermute(own, "core", [(0, 1), (1, 0)])
    outs = pl.pallas_call(
        attend_kernel,
        out_shape=jax.ShapeDtypeStruct((CHIPS, OUT_ROWS, D), bf16),
        in_specs=[SMEM, SMEM, VMEM, VMEM],
        out_specs=VMEM,
        compiler_params=PARAMS,
    )(block_mask, finished, own, peer)
    back = lax.all_to_all(outs, PLANE, 0, 0, tiled=True)
    return pl.pallas_call(
        finish_kernel,
        out_shape=(
            jax.ShapeDtypeStruct((1, TOK, HD), bf16),
            jax.ShapeDtypeStruct((HALF, 3 * D), bf16),
            jax.ShapeDtypeStruct((HALF, 3 * D), bf16),
        ),
        in_specs=[SMEM, VMEM, VMEM],
        out_specs=(VMEM, VMEM, VMEM),
        compiler_params=PARAMS,
    )(noise_step, back, gate_table)


def solution(mesh):
    fine = Mesh(mesh.devices.reshape(2, 4, 2, 2, 4), ("xl", "y", "core", "xh", "z"))
    span, patch = ("xl", "y", "core"), ("xh", "z")
    rows = P(span, patch, None)
    return jax.shard_map(
        on_device,
        mesh=fine,
        in_specs=(rows, rows, rows, P(), P(), P(), P(span), P(), P()),
        out_specs=(rows, P(span, patch), P(span, patch)),
        check_vma=False,
    )
```

```python
import math

import jax
import jax.numpy as jnp
from jax import lax
from jax.experimental import pallas as pl
from jax.experimental.pallas import tpu as pltpu
from jax.sharding import Mesh
from jax.sharding import PartitionSpec as P

D = 128
HEADS = 24
HD = HEADS * D
SPANS = 16
TOK = 64
HALF = TOK // 2
SLOTS = 32
CHIPS = 2 * SLOTS
ROWS = 2 * TOK + HALF
OUT_ROWS = 2 * HALF
PLANE = ("xl", "y", "xh", "z")
EPS = 1e-06
SCALE = D ** (-0.5)
SCALE_LOG2 = SCALE * math.log2(math.e)
Q_ROWS = 8 * HALF
BATCH = 4
LEAST, LARGEST = 2.0**-60, 2.0**100
NT = (((1,), (1,)), ((), ()))
VMEM = pl.BlockSpec(memory_space=pltpu.VMEM)
HBM = pl.BlockSpec(memory_space=pltpu.HBM)
SMEM = pl.BlockSpec(memory_space=pltpu.SMEM)


def head_slot():
    return lax.axis_index("y") * 8 + patch_index()


def patch_index():
    return lax.axis_index("xh") * 4 + lax.axis_index("z")


def pack_kernel(q_hbm, k_hbm, v_hbm, qg_hbm, kg_hbm, out_ref, q_ref, k_ref, v_ref, q_gain, k_gain, sems):
    copies = [
        pltpu.make_async_copy(src, dst, sems.at[i])
        for i, (src, dst) in enumerate(
            ((q_hbm, q_ref), (k_hbm, k_ref), (v_hbm, v_ref), (qg_hbm, q_gain), (kg_hbm, k_gain))
        )
    ]
    for copy in copies:
        copy.start()

    def factor(ref):
        wide = ref[0].astype(jnp.float32)
        return lax.rsqrt(jnp.mean(wide * wide, axis=-1, keepdims=True) + EPS)

    def normed(ref, scale, gain, h):
        wide = ref[0, :, h * D : (h + 1) * D].astype(jnp.float32)
        return (wide * scale * gain[h : h + 1, :]).astype(jnp.bfloat16)

    copies[0].wait()
    q_factor = factor(q_ref)
    copies[1].wait()
    k_factor = factor(k_ref)
    for copy in copies[2:]:
        copy.wait()
    for h in range(HEADS):
        qn = normed(q_ref, q_factor, q_gain, h)
        kn = normed(k_ref, k_factor, k_gain, h)
        for x in range(2):
            out_ref[x * SLOTS + h, 0:TOK, :] = kn
            out_ref[x * SLOTS + h, TOK : 2 * TOK, :] = v_ref[0, :, h * D : (h + 1) * D]
            out_ref[x * SLOTS + h, 2 * TOK : ROWS, :] = qn[x * HALF : (x + 1) * HALF]


def q_rows(ref, t):
    return ref[pl.ds(t * 8, 8), 2 * TOK : ROWS, :].reshape(Q_ROWS, D)


def span_keys(ref, u):
    return ref[pl.ds(u * 8, 8), 0:TOK, :].reshape(8 * TOK, D)


def span_values(ref, u):
    return ref[pl.ds(u * 8, 8), TOK : 2 * TOK, :].reshape(8 * TOK, D)


def first_counted(mask_ref, c):
    counted = mask_ref[c, 0]
    for j in range(1, SPANS):
        counted = counted + mask_ref[c, j]
    return c + 1 - counted


def own_range(mask_ref, core, t):
    first = first_counted(mask_ref, 2 * t + core)
    return (first - core + 1) // 2, t + 1


def peer_range(mask_ref, core, t):
    first = first_counted(mask_ref, 2 * t + core)
    return (first + core) // 2, t + core


def accumulate(bounds, q_ref, kv_ref, acc_ref, tot_ref, list_ref):
    n = jnp.int32(0)
    for t in range(8):
        low, high = bounds(t)

        def note(u, at, t=t):
            list_ref[0, at] = t
            list_ref[1, at] = t
            list_ref[2, at] = u
            return at + 1

        n = lax.fori_loop(low, high, note, n)
    for i in range(BATCH - 1):
        list_ref[0, n + i] = 0
        list_ref[1, n + i] = 8
        list_ref[2, n + i] = 0

    def batch(b, carry):
        for i in range(BATCH):
            at = b * BATCH + i
            u = list_ref[2, at]
            scores = lax.dot_general(
                q_rows(q_ref, list_ref[0, at]), span_keys(kv_ref, u), NT, preferred_element_type=jnp.float32
            )
            weight = jnp.exp2(scores * SCALE_LOG2)
            part = weight[:, 0:D]
            for k in range(1, 4):
                part = part + weight[:, k * D : (k + 1) * D]
            added = jnp.dot(weight.astype(jnp.bfloat16), span_values(kv_ref, u), preferred_element_type=jnp.float32)
            row = list_ref[1, at]
            acc_ref[row] += added
            tot_ref[row] += part
        return carry

    lax.fori_loop(0, (n + BATCH - 1) // BATCH, batch, 0)


def own_kernel(mask_ref, own_ref, acc_ref, tot_ref, list_ref):
    core = lax.axis_index("core")

    @pl.when(head_slot() < HEADS)
    def _():
        acc_ref[...] = jnp.zeros_like(acc_ref)
        tot_ref[...] = jnp.zeros_like(tot_ref)
        accumulate(lambda t: own_range(mask_ref, core, t), own_ref, own_ref, acc_ref, tot_ref, list_ref)


def peer_kernel(mask_ref, fin_ref, own_ref, peer_ref, acc_in, tot_in, out_ref, acc_ref, tot_ref, list_ref):
    core = lax.axis_index("core")
    xl = lax.axis_index("xl")
    head = head_slot()

    def shifted_block(q, ref, u, state):
        most, total, summed = state
        scores = lax.dot_general(q, span_keys(ref, u), NT, preferred_element_type=jnp.float32) * SCALE
        newest = jnp.maximum(most, jnp.max(scores, axis=1, keepdims=True))
        weight = jnp.exp(scores - newest)
        factor = jnp.exp(most - newest)
        total = total * factor + jnp.sum(weight, axis=1, keepdims=True)
        added = jnp.dot(weight.astype(jnp.bfloat16), span_values(ref, u), preferred_element_type=jnp.float32)
        return newest, total, summed * factor + added

    def shifted_span(t, carry):
        q = q_rows(own_ref, t)
        state = (
            jnp.full((Q_ROWS, 1), -1e30, jnp.float32),
            jnp.zeros((Q_ROWS, 1), jnp.float32),
            jnp.zeros((Q_ROWS, D), jnp.float32),
        )
        low, high = own_range(mask_ref, core, t)
        state = lax.fori_loop(low, high, lambda u, s: shifted_block(q, own_ref, u, s), state)
        low, high = peer_range(mask_ref, core, t)
        state = lax.fori_loop(low, high, lambda u, s: shifted_block(q, peer_ref, u, s), state)
        _, total, summed = state
        out_ref[pl.ds(t * 8, 8), 0:HALF, :] = (summed / total).astype(jnp.bfloat16).reshape(8, HALF, D)
        return carry

    @pl.when(head < HEADS)
    def _():
        acc_ref[...] = acc_in[...]
        tot_ref[...] = tot_in[...]
        accumulate(lambda t: peer_range(mask_ref, core, t), own_ref, peer_ref, acc_ref, tot_ref, list_ref)
        least = jnp.full((Q_ROWS, 1), 1.0, jnp.float32)
        largest = least
        for t in range(8):
            total = jnp.sum(tot_ref[t], axis=1, keepdims=True)
            least = jnp.minimum(least, total)
            largest = jnp.maximum(largest, total)
            attn = acc_ref[t] * (1.0 / total)
            out_ref[t * 8 : (t + 1) * 8, 0:HALF, :] = attn.astype(jnp.bfloat16).reshape(8, HALF, D)
        sound = jnp.logical_and(jnp.min(least) >= LEAST, jnp.max(largest) <= LARGEST)

        @pl.when(jnp.logical_not(sound))
        def _():
            lax.fori_loop(0, 8, shifted_span, 0)

        fin = fin_ref[0]
        column = head // 3
        start = core * HALF + xl * (HALF // 2)

        def commit(ref):
            for t in range(8):
                slot = (fin // 2) * 8 + t
                for i in range(2):
                    rows = ref[slot, pl.ds(pl.multiple_of(start + i * TOK, 16), HALF // 2), :]
                    out_ref[t * 8 + column, pl.ds(HALF + i * (HALF // 2), HALF // 2), :] = rows

        pl.when(fin % 2 == core)(lambda: commit(own_ref))
        pl.when(fin % 2 != core)(lambda: commit(peer_ref))


def finish_kernel(step_ref, in_ref, gate_ref, mixed_ref, k_ref, v_ref):
    gate = gate_ref[pl.ds(step_ref[0], 1), :]
    for h in range(HEADS):
        cols = slice(h * D, (h + 1) * D)
        for x in range(2):
            rows = slice(x * HALF, (x + 1) * HALF)
            attn = in_ref[x * SLOTS + h, 0:HALF, :].astype(jnp.float32)
            mixed_ref[0, rows, cols] = (attn * gate[:, cols]).astype(jnp.bfloat16)
    patch = patch_index()
    for i in range(3):
        for x in range(2):
            src = x * SLOTS + 3 * patch + i
            rows = slice(x * (HALF // 2), (x + 1) * (HALF // 2))
            k_ref[rows, i * D : (i + 1) * D] = in_ref[src, HALF : HALF + HALF // 2, :]
            v_ref[rows, i * D : (i + 1) * D] = in_ref[src, HALF + HALF // 2 : OUT_ROWS, :]


PARAMS = pltpu.CompilerParams(vmem_limit_bytes=32 * 1024 * 1024)


def on_device(queries, keys, values, q_gain, k_gain, gate_table, noise_step, block_mask, finished):
    bf16 = jnp.bfloat16
    f32 = jnp.float32
    packed = pl.pallas_call(
        pack_kernel,
        out_shape=jax.ShapeDtypeStruct((CHIPS, ROWS, D), bf16),
        in_specs=[HBM] * 5,
        out_specs=VMEM,
        scratch_shapes=[pltpu.VMEM((1, TOK, HD), bf16)] * 3
        + [pltpu.VMEM((HEADS, D), f32)] * 2
        + [pltpu.SemaphoreType.DMA((5,))],
        compiler_params=pltpu.CompilerParams(vmem_limit_bytes=60 * 1024 * 1024),
    )(queries, keys, values, q_gain.reshape(HEADS, D), k_gain.reshape(HEADS, D))
    own = lax.all_to_all(packed, PLANE, 0, 0, tiled=True)
    peer = lax.ppermute(own, "core", [(0, 1), (1, 0)])
    sums = [jax.ShapeDtypeStruct((9, Q_ROWS, D), f32)] * 2
    blocks = pltpu.SMEM((3, 64), jnp.int32)
    acc, tot = pl.pallas_call(
        own_kernel,
        out_shape=sums,
        in_specs=[SMEM, VMEM],
        out_specs=[VMEM, VMEM],
        scratch_shapes=[blocks],
        compiler_params=PARAMS,
        cost_estimate=pl.CostEstimate(flops=2**31, bytes_accessed=2**22, transcendentals=2**22),
    )(block_mask, own)
    outs = pl.pallas_call(
        peer_kernel,
        out_shape=jax.ShapeDtypeStruct((CHIPS, OUT_ROWS, D), bf16),
        in_specs=[SMEM, SMEM, VMEM, VMEM, VMEM, VMEM],
        out_specs=VMEM,
        scratch_shapes=[pltpu.VMEM((9, Q_ROWS, D), f32)] * 2 + [blocks],
        compiler_params=PARAMS,
    )(block_mask, finished, own, peer, acc, tot)
    back = lax.all_to_all(outs, PLANE, 0, 0, tiled=True)
    return pl.pallas_call(
        finish_kernel,
        out_shape=(
            jax.ShapeDtypeStruct((1, TOK, HD), bf16),
            jax.ShapeDtypeStruct((HALF, 3 * D), bf16),
            jax.ShapeDtypeStruct((HALF, 3 * D), bf16),
        ),
        in_specs=[SMEM, VMEM, VMEM],
        out_specs=(VMEM, VMEM, VMEM),
        compiler_params=PARAMS,
    )(noise_step, back, gate_table)


def solution(mesh):
    fine = Mesh(mesh.devices.reshape(2, 4, 2, 2, 4), ("xl", "y", "core", "xh", "z"))
    span, patch = ("xl", "y", "core"), ("xh", "z")
    rows = P(span, patch, None)
    return jax.shard_map(
        on_device,
        mesh=fine,
        in_specs=(rows, rows, rows, P(), P(), P(), P(span), P(), P()),
        out_specs=(rows, P(span, patch), P(span, patch)),
        check_vma=False,
    )
```

```python
import math

import jax
import jax.numpy as jnp
from jax import lax
from jax.experimental import pallas as pl
from jax.experimental.pallas import tpu as pltpu
from jax.sharding import Mesh
from jax.sharding import PartitionSpec as P

D = 128
HEADS = 24
HD = HEADS * D
SPANS = 16
TOK = 64
HALF = TOK // 2
SLOTS = 32
CHIPS = 2 * SLOTS
ROWS = 2 * TOK + HALF
SPARE = 12
PART = HALF // 2
SPARE_ROWS = 8 * PART
PLANE = ("xl", "y", "xh", "z")
EPS = 1e-06
SCALE = D ** (-0.5)
SCALE_LOG2 = SCALE * math.log2(math.e)
Q_ROWS = 8 * HALF
GROUP = 4
BATCH = 4
LEAST, LARGEST = 2.0**-60, 2.0**100
NT = (((1,), (1,)), ((), ()))
VMEM = pl.BlockSpec(memory_space=pltpu.VMEM)
ANY = pl.BlockSpec(memory_space=pl.ANY)
HBM = pl.BlockSpec(memory_space=pltpu.HBM)
SMEM = pl.BlockSpec(memory_space=pltpu.SMEM)


def head_slot():
    return lax.axis_index("y") * 8 + patch_index()


def patch_index():
    return lax.axis_index("xh") * 4 + lax.axis_index("z")


def normed(ref, scale, gain, h):
    wide = ref[:, h * D : (h + 1) * D].astype(jnp.float32)
    return (wide * scale * gain[h : h + 1, :]).astype(jnp.bfloat16)


def norm_factor(ref):
    wide = ref[...].astype(jnp.float32)
    return lax.rsqrt(jnp.mean(wide * wide, axis=-1, keepdims=True) + EPS)


def pack_kernel(q_hbm, k_hbm, v_hbm, qg_hbm, kg_hbm, out_hbm, q_ref, k_ref, v_ref, q_gain, k_gain, out_ref, sems, out_sems):
    copies = [
        pltpu.make_async_copy(src, dst, sems.at[i])
        for i, (src, dst) in enumerate(
            ((q_hbm.at[0], q_ref), (k_hbm.at[0], k_ref), (v_hbm.at[0], v_ref), (qg_hbm, q_gain), (kg_hbm, k_gain))
        )
    ]
    for copy in copies:
        copy.start()
    copies[0].wait()
    q_factor = norm_factor(q_ref)
    copies[1].wait()
    k_factor = norm_factor(k_ref)
    for copy in copies[2:]:
        copy.wait()
    sent = []
    for h in range(HEADS):
        qn = normed(q_ref, q_factor, q_gain, h)
        kn = normed(k_ref, k_factor, k_gain, h)
        for x in range(2):
            out_ref[x * SLOTS + h, 0:TOK, :] = kn
            out_ref[x * SLOTS + h, TOK : 2 * TOK, :] = v_ref[:, h * D : (h + 1) * D]
            out_ref[x * SLOTS + h, 2 * TOK : ROWS, :] = qn[x * HALF : (x + 1) * HALF]
        if h % GROUP == GROUP - 1:
            for x in range(2):
                group = pl.ds(x * SLOTS + h + 1 - GROUP, GROUP)
                sent.append(pltpu.make_async_copy(out_ref.at[group], out_hbm.at[group], out_sems.at[len(sent)]))
                sent[-1].start()
    for copy in sent:
        copy.wait()


def spare_kernel(fin_ref, k_own, v_own, k_peer, v_peer, kg_hbm, packed, out_hbm, k_ref, v_ref, k_gain, stage, sems):
    fin = fin_ref[0]
    core = lax.axis_index("core")
    rows = pl.ds(pl.multiple_of(core * HALF, HALF), HALF)

    @pl.when(fin // 2 == lax.axis_index("xl") * 4 + lax.axis_index("y"))
    def _():
        def fetch(k_hbm, v_hbm):
            copies = [
                pltpu.make_async_copy(src, dst, sems.at[i])
                for i, (src, dst) in enumerate(((k_hbm.at[0, rows], k_ref), (v_hbm.at[0, rows], v_ref), (kg_hbm, k_gain)))
            ]
            for copy in copies:
                copy.start()
            for copy in copies:
                copy.wait()

        pl.when(fin % 2 == core)(lambda: fetch(k_own, v_own))
        pl.when(fin % 2 != core)(lambda: fetch(k_peer, v_peer))
        factor = norm_factor(k_ref)
        for p in range(8):
            for i in range(3):
                h = 3 * p + i
                kn = normed(k_ref, factor, k_gain, h)
                vn = v_ref[:, h * D : (h + 1) * D]
                for half in range(2):
                    part = slice(half * PART, (half + 1) * PART)
                    stage[i * 4 + half, p * PART : (p + 1) * PART, :] = kn[part]
                    stage[i * 4 + 2 + half, p * PART : (p + 1) * PART, :] = vn[part]
        copies = [
            pltpu.make_async_copy(stage.at[pl.ds(0, 8)], out_hbm.at[pl.ds(HEADS, 8), pl.ds(0, SPARE_ROWS)], sems.at[3]),
            pltpu.make_async_copy(
                stage.at[pl.ds(8, SPARE - 8)], out_hbm.at[pl.ds(SLOTS + HEADS, SPARE - 8), pl.ds(0, SPARE_ROWS)], sems.at[4]
            ),
        ]
        for copy in copies:
            copy.start()
        for copy in copies:
            copy.wait()


def spare_slot(e):
    return HEADS + e if e < 8 else SLOTS + HEADS + e - 8


def q_rows(ref, t):
    return ref[pl.ds(t * 8, 8), 2 * TOK : ROWS, :].reshape(Q_ROWS, D)


def span_keys(ref, u):
    return ref[pl.ds(u * 8, 8), 0:TOK, :].reshape(8 * TOK, D)


def span_values(ref, u):
    return ref[pl.ds(u * 8, 8), TOK : 2 * TOK, :].reshape(8 * TOK, D)


def first_counted(mask_ref, c):
    counted = mask_ref[c, 0]
    for j in range(1, SPANS):
        counted = counted + mask_ref[c, j]
    return c + 1 - counted


def own_range(mask_ref, core, t):
    first = first_counted(mask_ref, 2 * t + core)
    return (first - core + 1) // 2, t + 1


def peer_range(mask_ref, core, t):
    first = first_counted(mask_ref, 2 * t + core)
    return (first + core) // 2, t + core


def accumulate(bounds, q_ref, kv_ref, acc_ref, tot_ref, list_ref):
    n = jnp.int32(0)
    for t in range(8):
        low, high = bounds(t)

        def note(u, at, t=t):
            list_ref[0, at] = t
            list_ref[1, at] = t
            list_ref[2, at] = u
            return at + 1

        n = lax.fori_loop(low, high, note, n)
    for i in range(BATCH - 1):
        list_ref[0, n + i] = 0
        list_ref[1, n + i] = 8
        list_ref[2, n + i] = 0

    def batch(b, carry):
        for i in range(BATCH):
            at = b * BATCH + i
            u = list_ref[2, at]
            scores = lax.dot_general(
                q_rows(q_ref, list_ref[0, at]), span_keys(kv_ref, u), NT, preferred_element_type=jnp.float32
            )
            weight = jnp.exp2(scores * SCALE_LOG2)
            part = weight[:, 0:D]
            for k in range(1, 4):
                part = part + weight[:, k * D : (k + 1) * D]
            added = jnp.dot(weight.astype(jnp.bfloat16), span_values(kv_ref, u), preferred_element_type=jnp.float32)
            row = list_ref[1, at]
            acc_ref[row] += added
            tot_ref[row] += part
        return carry

    lax.fori_loop(0, (n + BATCH - 1) // BATCH, batch, 0)


def own_kernel(mask_ref, own_ref, acc_ref, tot_ref, list_ref):
    core = lax.axis_index("core")

    @pl.when(head_slot() < HEADS)
    def _():
        acc_ref[...] = jnp.zeros_like(acc_ref)
        tot_ref[...] = jnp.zeros_like(tot_ref)
        accumulate(lambda t: own_range(mask_ref, core, t), own_ref, own_ref, acc_ref, tot_ref, list_ref)


def peer_kernel(mask_ref, fin_ref, own_ref, peer_ref, acc_in, tot_in, out_ref, acc_ref, tot_ref, list_ref):
    core = lax.axis_index("core")
    xl = lax.axis_index("xl")
    head = head_slot()

    def shifted_block(q, ref, u, state):
        most, total, summed = state
        scores = lax.dot_general(q, span_keys(ref, u), NT, preferred_element_type=jnp.float32) * SCALE
        newest = jnp.maximum(most, jnp.max(scores, axis=1, keepdims=True))
        weight = jnp.exp(scores - newest)
        factor = jnp.exp(most - newest)
        total = total * factor + jnp.sum(weight, axis=1, keepdims=True)
        added = jnp.dot(weight.astype(jnp.bfloat16), span_values(ref, u), preferred_element_type=jnp.float32)
        return newest, total, summed * factor + added

    def shifted_span(t, carry):
        q = q_rows(own_ref, t)
        state = (
            jnp.full((Q_ROWS, 1), -1e30, jnp.float32),
            jnp.zeros((Q_ROWS, 1), jnp.float32),
            jnp.zeros((Q_ROWS, D), jnp.float32),
        )
        low, high = own_range(mask_ref, core, t)
        state = lax.fori_loop(low, high, lambda u, s: shifted_block(q, own_ref, u, s), state)
        low, high = peer_range(mask_ref, core, t)
        state = lax.fori_loop(low, high, lambda u, s: shifted_block(q, peer_ref, u, s), state)
        _, total, summed = state
        out_ref[pl.ds(t * 8, 8), 0:HALF, :] = (summed / total).astype(jnp.bfloat16).reshape(8, HALF, D)
        return carry

    @pl.when(head < HEADS)
    def _():
        acc_ref[...] = acc_in[...]
        tot_ref[...] = tot_in[...]
        accumulate(lambda t: peer_range(mask_ref, core, t), own_ref, peer_ref, acc_ref, tot_ref, list_ref)
        least = jnp.full((Q_ROWS, 1), 1.0, jnp.float32)
        largest = least
        for t in range(8):
            total = jnp.sum(tot_ref[t], axis=1, keepdims=True)
            least = jnp.minimum(least, total)
            largest = jnp.maximum(largest, total)
            attn = acc_ref[t] * (1.0 / total)
            out_ref[t * 8 : (t + 1) * 8, 0:HALF, :] = attn.astype(jnp.bfloat16).reshape(8, HALF, D)
        sound = jnp.logical_and(jnp.min(least) >= LEAST, jnp.max(largest) <= LARGEST)

        @pl.when(jnp.logical_not(sound))
        def _():
            lax.fori_loop(0, 8, shifted_span, 0)

    @pl.when(jnp.logical_and(head >= HEADS, xl * 8 + head - HEADS < SPARE))
    def _():
        fin = fin_ref[0]
        for t in range(8):
            for p in range(8):
                out_ref[t * 8 + p, 0:PART, :] = own_ref[(fin // 2) * 8 + t, p * PART : (p + 1) * PART, :]


def finish_kernel(step_ref, in_ref, gate_ref, mixed_ref, k_ref, v_ref):
    gate = gate_ref[pl.ds(step_ref[0], 1), :]
    for h in range(HEADS):
        cols = slice(h * D, (h + 1) * D)
        for x in range(2):
            rows = slice(x * HALF, (x + 1) * HALF)
            attn = in_ref[x * SLOTS + h, 0:HALF, :].astype(jnp.float32)
            mixed_ref[0, rows, cols] = (attn * gate[:, cols]).astype(jnp.bfloat16)
    for e in range(SPARE):
        i, half = e // 4, e % 2
        ref = k_ref if e % 4 < 2 else v_ref
        ref[half * PART : (half + 1) * PART, i * D : (i + 1) * D] = in_ref[spare_slot(e), 0:PART, :]


PARAMS = pltpu.CompilerParams(vmem_limit_bytes=32 * 1024 * 1024)

WIDE = pltpu.CompilerParams(vmem_limit_bytes=60 * 1024 * 1024)


def on_device(queries, keys, values, q_gain, k_gain, gate_table, noise_step, block_mask, finished):
    bf16 = jnp.bfloat16
    f32 = jnp.float32
    gain = k_gain.reshape(HEADS, D)
    swap = [(0, 1), (1, 0)]
    k_peer = lax.ppermute(keys, "core", swap)
    v_peer = lax.ppermute(values, "core", swap)
    packed = pl.pallas_call(
        pack_kernel,
        out_shape=jax.ShapeDtypeStruct((CHIPS, ROWS, D), bf16),
        in_specs=[HBM] * 5,
        out_specs=HBM,
        scratch_shapes=[pltpu.VMEM((TOK, HD), bf16)] * 3
        + [pltpu.VMEM((HEADS, D), f32)] * 2
        + [pltpu.VMEM((CHIPS, ROWS, D), bf16)]
        + [pltpu.SemaphoreType.DMA((5,)), pltpu.SemaphoreType.DMA((2 * HEADS // GROUP,))],
        compiler_params=WIDE,
        cost_estimate=pl.CostEstimate(flops=2**24, bytes_accessed=2**23, transcendentals=0),
    )(queries, keys, values, q_gain.reshape(HEADS, D), gain)
    packed = pl.pallas_call(
        spare_kernel,
        out_shape=jax.ShapeDtypeStruct((CHIPS, ROWS, D), bf16),
        in_specs=[SMEM, HBM, HBM, ANY, ANY, HBM, HBM],
        out_specs=HBM,
        scratch_shapes=[pltpu.VMEM((HALF, HD), bf16)] * 2
        + [pltpu.VMEM((HEADS, D), f32), pltpu.VMEM((SPARE, SPARE_ROWS, D), bf16), pltpu.SemaphoreType.DMA((5,))],
        input_output_aliases={6: 0},
        compiler_params=pltpu.CompilerParams(vmem_limit_bytes=48 * 1024 * 1024),
    )(finished, keys, values, k_peer, v_peer, gain, packed)
    own = lax.all_to_all(packed, PLANE, 0, 0, tiled=True)
    peer = lax.ppermute(own, "core", swap)
    sums = [jax.ShapeDtypeStruct((9, Q_ROWS, D), f32)] * 2
    blocks = pltpu.SMEM((3, 64), jnp.int32)
    acc, tot = pl.pallas_call(
        own_kernel,
        out_shape=sums,
        in_specs=[SMEM, VMEM],
        out_specs=[VMEM, VMEM],
        scratch_shapes=[blocks],
        compiler_params=PARAMS,
        cost_estimate=pl.CostEstimate(flops=2**31, bytes_accessed=2**22, transcendentals=2**22),
    )(block_mask, own)
    outs = pl.pallas_call(
        peer_kernel,
        out_shape=jax.ShapeDtypeStruct((CHIPS, HALF, D), bf16),
        in_specs=[SMEM, SMEM, VMEM, VMEM, VMEM, VMEM],
        out_specs=VMEM,
        scratch_shapes=[pltpu.VMEM((9, Q_ROWS, D), f32)] * 2 + [blocks],
        compiler_params=PARAMS,
    )(block_mask, finished, own, peer, acc, tot)
    back = lax.all_to_all(outs, PLANE, 0, 0, tiled=True)
    return pl.pallas_call(
        finish_kernel,
        out_shape=(
            jax.ShapeDtypeStruct((1, TOK, HD), bf16),
            jax.ShapeDtypeStruct((HALF, 3 * D), bf16),
            jax.ShapeDtypeStruct((HALF, 3 * D), bf16),
        ),
        in_specs=[SMEM, VMEM, VMEM],
        out_specs=(VMEM, VMEM, VMEM),
        compiler_params=PARAMS,
    )(noise_step, back, gate_table)


def solution(mesh):
    fine = Mesh(mesh.devices.reshape(2, 4, 2, 2, 4), ("xl", "y", "core", "xh", "z"))
    span, patch = ("xl", "y", "core"), ("xh", "z")
    rows = P(span, patch, None)
    return jax.shard_map(
        on_device,
        mesh=fine,
        in_specs=(rows, rows, rows, P(), P(), P(), P(span), P(), P()),
        out_specs=(rows, P(span, patch), P(span, patch)),
        check_vma=False,
    )
```

```python
import math

import jax
import jax.numpy as jnp
from jax import lax
from jax.experimental import pallas as pl
from jax.experimental.pallas import tpu as pltpu
from jax.sharding import Mesh
from jax.sharding import PartitionSpec as P

D = 128
HEADS = 24
HD = HEADS * D
SPANS = 16
TOK = 64
HALF = TOK // 2
SLOTS = 32
CHIPS = 2 * SLOTS
ROWS = 2 * TOK + HALF
SPARE = 12
PART = HALF // 2
PLANE = ("xl", "y", "xh", "z")
EPS = 1e-06
SCALE = D ** (-0.5)
SCALE_LOG2 = SCALE * math.log2(math.e)
Q_ROWS = 8 * HALF
BATCH = 2
LEAST, LARGEST = 2.0**-60, 2.0**100
NT = (((1,), (1,)), ((), ()))
VMEM = pl.BlockSpec(memory_space=pltpu.VMEM)
ANY = pl.BlockSpec(memory_space=pl.ANY)
SMEM = pl.BlockSpec(memory_space=pltpu.SMEM)


def head_slot():
    return lax.axis_index("y") * 8 + patch_index()


def patch_index():
    return lax.axis_index("xh") * 4 + lax.axis_index("z")


def normed(ref, rows, factor, gain, h):
    wide = ref[0, rows, h * D : (h + 1) * D].astype(jnp.float32)
    return (wide * factor * gain[h : h + 1, :]).astype(jnp.bfloat16)


def norm_factor(block):
    wide = block.astype(jnp.float32)
    return lax.rsqrt(jnp.mean(wide * wide, axis=-1, keepdims=True) + EPS)


def pack_kernel(fin_ref, q_ref, k_ref, v_ref, k_peer, v_peer, q_gain, k_gain, out_ref):
    q_factor = norm_factor(q_ref[0])
    k_factor = norm_factor(k_ref[0])
    for h in range(HEADS):
        qn = normed(q_ref, slice(None), q_factor, q_gain, h)
        kn = normed(k_ref, slice(None), k_factor, k_gain, h)
        for x in range(2):
            out_ref[x * SLOTS + h, 0:TOK, :] = kn
            out_ref[x * SLOTS + h, TOK : 2 * TOK, :] = v_ref[0, :, h * D : (h + 1) * D]
            out_ref[x * SLOTS + h, 2 * TOK : ROWS, :] = qn[x * HALF : (x + 1) * HALF]

    fin = fin_ref[0]
    core = lax.axis_index("core")
    rows = pl.ds(pl.multiple_of(core * HALF, HALF), HALF)

    def spare(k_half, v_half):
        factor = norm_factor(k_half[0, rows, :])
        for p in range(8):
            part = slice(p * PART, (p + 1) * PART)
            for i in range(3):
                h = 3 * p + i
                kn = normed(k_half, rows, factor, k_gain, h)
                vn = v_half[0, rows, h * D : (h + 1) * D]
                for half in range(2):
                    out_ref[spare_slot(i * 4 + half), part, :] = kn[half * PART : (half + 1) * PART]
                    out_ref[spare_slot(i * 4 + 2 + half), part, :] = vn[half * PART : (half + 1) * PART]

    here = fin // 2 == lax.axis_index("xl") * 4 + lax.axis_index("y")
    pl.when(jnp.logical_and(here, fin % 2 == core))(lambda: spare(k_ref, v_ref))
    pl.when(jnp.logical_and(here, fin % 2 != core))(lambda: spare(k_peer, v_peer))


def spare_slot(e):
    return HEADS + e if e < 8 else SLOTS + HEADS + e - 8


def q_rows(ref, t):
    return ref[pl.ds(t * 8, 8), 2 * TOK : ROWS, :].reshape(Q_ROWS, D)


def span_keys(ref, u, spans=1):
    return ref[pl.ds(u * 8, spans * 8), 0:TOK, :].reshape(spans * 8 * TOK, D)


def span_values(ref, u, spans=1):
    return ref[pl.ds(u * 8, spans * 8), TOK : 2 * TOK, :].reshape(spans * 8 * TOK, D)


def first_counted(mask_ref, core, t):
    c = 2 * t + core
    counted = mask_ref[c, 0]
    for j in range(1, 2 * t + 2 if isinstance(t, int) else SPANS):
        counted = counted + mask_ref[c, j]
    return c + 1 - counted


def own_range(first, core, t):
    return jnp.right_shift(first - core + 1, 1), t + 1


def peer_range(first, core, t):
    return jnp.right_shift(first + core, 1), t + core


def list_kernel(mask_any, list_ref, mask_ref, sem):
    copy = pltpu.make_async_copy(mask_any, mask_ref, sem.at[0])
    copy.start()
    core = lax.axis_index("core")
    copy.wait()
    firsts = [first_counted(mask_ref, core, t) for t in range(8)]
    for at, bounds in ((0, own_range), (4, peer_range)):
        pairs = singles = jnp.int32(0)
        for t in range(8):
            low, high = bounds(firsts[t], core, t)
            count = high - low
            list_ref[at + 2, singles] = t
            list_ref[at + 3, singles] = high - 1
            singles = singles + jnp.bitwise_and(count, 1)

            def note(i, n, t=t, low=low, at=at):
                list_ref[at, n] = t
                list_ref[at + 1, n] = low + 2 * i
                return n + 1

            pairs = lax.fori_loop(0, jnp.right_shift(count, 1), note, pairs)
        for row, total in ((at, pairs), (at + 2, singles)):
            list_ref[row, total] = 8
            list_ref[row + 1, total] = 0
            list_ref[row, 63] = total


def accumulate(list_ref, at, q_ref, kv_ref, acc_ref, tot_ref):
    def block(row, u, spans):
        q = q_rows(q_ref, jnp.minimum(row, 7))
        scores = lax.dot_general(q, span_keys(kv_ref, u, spans), NT, preferred_element_type=jnp.float32)
        weight = jnp.exp2(scores * SCALE_LOG2)
        part = weight[:, 0:D]
        for k in range(1, spans * 8 * TOK // D):
            part = part + weight[:, k * D : (k + 1) * D]
        added = jnp.dot(weight.astype(jnp.bfloat16), span_values(kv_ref, u, spans), preferred_element_type=jnp.float32)
        acc_ref[row] += added
        tot_ref[row] += part

    for spans, line in ((2, at), (1, at + 2)):

        def step(b, carry, spans=spans, line=line):
            for i in range(BATCH):
                block(list_ref[line, b * BATCH + i], list_ref[line + 1, b * BATCH + i], spans)
            return carry

        lax.fori_loop(0, (list_ref[line, 63] + BATCH - 1) // BATCH, step, 0)


def own_kernel(list_ref, own_ref, acc_ref, tot_ref):
    @pl.when(head_slot() < HEADS)
    def _():
        acc_ref[...] = jnp.zeros_like(acc_ref)
        tot_ref[...] = jnp.zeros_like(tot_ref)
        accumulate(list_ref, 0, own_ref, own_ref, acc_ref, tot_ref)


def peer_kernel(mask_any, fin_ref, list_ref, own_ref, peer_ref, acc_in, tot_in, out_ref, acc_ref, tot_ref, mask_ref, sem):
    core = lax.axis_index("core")
    xl = lax.axis_index("xl")
    head = head_slot()

    def shifted_block(q, ref, u, state):
        most, total, summed = state
        scores = lax.dot_general(q, span_keys(ref, u), NT, preferred_element_type=jnp.float32) * SCALE
        newest = jnp.maximum(most, jnp.max(scores, axis=1, keepdims=True))
        weight = jnp.exp(scores - newest)
        factor = jnp.exp(most - newest)
        total = total * factor + jnp.sum(weight, axis=1, keepdims=True)
        added = jnp.dot(weight.astype(jnp.bfloat16), span_values(ref, u), preferred_element_type=jnp.float32)
        return newest, total, summed * factor + added

    def shifted_span(t, carry):
        q = q_rows(own_ref, t)
        state = (
            jnp.full((Q_ROWS, 1), -1e30, jnp.float32),
            jnp.zeros((Q_ROWS, 1), jnp.float32),
            jnp.zeros((Q_ROWS, D), jnp.float32),
        )
        first = first_counted(mask_ref, core, t)
        low, high = own_range(first, core, t)
        state = lax.fori_loop(low, high, lambda u, s: shifted_block(q, own_ref, u, s), state)
        low, high = peer_range(first, core, t)
        state = lax.fori_loop(low, high, lambda u, s: shifted_block(q, peer_ref, u, s), state)
        _, total, summed = state
        out_ref[pl.ds(t * 8, 8), 0:HALF, :] = (summed / total).astype(jnp.bfloat16).reshape(8, HALF, D)
        return carry

    @pl.when(head < HEADS)
    def _():
        accumulate(list_ref, 4, own_ref, peer_ref, acc_ref, tot_ref)
        least = jnp.full((Q_ROWS, 1), 1.0, jnp.float32)
        largest = least
        for t in range(8):
            total = jnp.sum(tot_ref[t], axis=1, keepdims=True)
            least = jnp.minimum(least, total)
            largest = jnp.maximum(largest, total)
            attn = acc_ref[t] * (1.0 / total)
            out_ref[t * 8 : (t + 1) * 8, 0:HALF, :] = attn.astype(jnp.bfloat16).reshape(8, HALF, D)
        sound = jnp.logical_and(jnp.min(least) >= LEAST, jnp.max(largest) <= LARGEST)

        @pl.when(jnp.logical_not(sound))
        def _():
            copy = pltpu.make_async_copy(mask_any, mask_ref, sem.at[0])
            copy.start()
            copy.wait()
            lax.fori_loop(0, 8, shifted_span, 0)

    @pl.when(jnp.logical_and(head >= HEADS, xl * 8 + head - HEADS < SPARE))
    def _():
        fin = fin_ref[0]
        for t in range(8):
            for p in range(8):
                out_ref[t * 8 + p, 0:PART, :] = own_ref[(fin // 2) * 8 + t, p * PART : (p + 1) * PART, :]


def finish_kernel(step_ref, in_ref, gate_ref, mixed_ref, k_ref, v_ref):
    gate = gate_ref[pl.ds(step_ref[0], 1), :]
    for h in range(HEADS):
        cols = slice(h * D, (h + 1) * D)
        for x in range(2):
            rows = slice(x * HALF, (x + 1) * HALF)
            attn = in_ref[x * SLOTS + h, 0:HALF, :].astype(jnp.float32)
            mixed_ref[0, rows, cols] = (attn * gate[:, cols]).astype(jnp.bfloat16)
    for e in range(SPARE):
        i, half = e // 4, e % 2
        ref = k_ref if e % 4 < 2 else v_ref
        ref[half * PART : (half + 1) * PART, i * D : (i + 1) * D] = in_ref[spare_slot(e), 0:PART, :]


PARAMS = pltpu.CompilerParams(vmem_limit_bytes=32 * 1024 * 1024)


def on_device(queries, keys, values, q_gain, k_gain, gate_table, noise_step, block_mask, finished):
    bf16 = jnp.bfloat16
    f32 = jnp.float32
    swap = [(0, 1), (1, 0)]
    k_peer = lax.ppermute(keys, "core", swap)
    v_peer = lax.ppermute(values, "core", swap)
    lists = pl.pallas_call(
        list_kernel,
        out_shape=jax.ShapeDtypeStruct((8, 64), jnp.int32),
        in_specs=[ANY],
        out_specs=SMEM,
        scratch_shapes=[pltpu.SMEM((SPANS, SPANS), jnp.int32), pltpu.SemaphoreType.DMA((1,))],
        cost_estimate=pl.CostEstimate(flops=2**32, bytes_accessed=2**12, transcendentals=0),
    )(block_mask)
    k_peer, lists = lax.optimization_barrier((k_peer, lists))
    packed = pl.pallas_call(
        pack_kernel,
        out_shape=jax.ShapeDtypeStruct((CHIPS, ROWS, D), bf16),
        in_specs=[SMEM] + [VMEM] * 7,
        out_specs=VMEM,
        compiler_params=PARAMS,
    )(finished, queries, keys, values, k_peer, v_peer, q_gain.reshape(HEADS, D), k_gain.reshape(HEADS, D))
    own = lax.all_to_all(packed, PLANE, 0, 0, tiled=True)
    peer = lax.ppermute(own, "core", swap)
    sums = [jax.ShapeDtypeStruct((9, Q_ROWS, D), f32)] * 2
    acc, tot = pl.pallas_call(
        own_kernel,
        out_shape=sums,
        in_specs=[SMEM, VMEM],
        out_specs=[VMEM, VMEM],
        compiler_params=PARAMS,
        cost_estimate=pl.CostEstimate(flops=2**31, bytes_accessed=2**22, transcendentals=2**22),
    )(lists, own)
    outs, _, _ = pl.pallas_call(
        peer_kernel,
        out_shape=[jax.ShapeDtypeStruct((CHIPS, HALF, D), bf16)] + sums,
        in_specs=[ANY, SMEM, SMEM] + [VMEM] * 4,
        out_specs=[VMEM] * 3,
        scratch_shapes=[pltpu.SMEM((SPANS, SPANS), jnp.int32), pltpu.SemaphoreType.DMA((1,))],
        input_output_aliases={5: 1, 6: 2},
        compiler_params=PARAMS,
    )(block_mask, finished, lists, own, peer, acc, tot)
    back = lax.all_to_all(outs, PLANE, 0, 0, tiled=True)
    return pl.pallas_call(
        finish_kernel,
        out_shape=(
            jax.ShapeDtypeStruct((1, TOK, HD), bf16),
            jax.ShapeDtypeStruct((HALF, 3 * D), bf16),
            jax.ShapeDtypeStruct((HALF, 3 * D), bf16),
        ),
        in_specs=[SMEM, VMEM, VMEM],
        out_specs=(VMEM, VMEM, VMEM),
        compiler_params=PARAMS,
    )(noise_step, back, gate_table)


def solution(mesh):
    fine = Mesh(mesh.devices.reshape(2, 4, 2, 2, 4), ("xl", "y", "core", "xh", "z"))
    span, patch = ("xl", "y", "core"), ("xh", "z")
    rows = P(span, patch, None)
    return jax.shard_map(
        on_device,
        mesh=fine,
        in_specs=(rows, rows, rows, P(), P(), P(), P(span), P(), P()),
        out_specs=(rows, P(span, patch), P(span, patch)),
        check_vma=False,
    )
```

```python
import math

import jax
import jax.numpy as jnp
from jax import lax
from jax.experimental import pallas as pl
from jax.experimental.pallas import tpu as pltpu
from jax.sharding import Mesh
from jax.sharding import PartitionSpec as P

D = 128
HEADS = 24
HD = HEADS * D
SPANS = 16
TOK = 64
HALF = TOK // 2
SLOTS = 32
CHIPS = 2 * SLOTS
IDLE = SLOTS - HEADS
ROWS = 2 * TOK + HALF
SPARE = 12
PART = HALF // 2
PLANE = ("xl", "y", "xh", "z")
EPS = 1e-06
SCALE = D ** (-0.5)
SCALE_LOG2 = SCALE * math.log2(math.e)
Q_ROWS = 8 * HALF
LATER = 2
BATCH = 2
LEAST, LARGEST = 2.0**-60, 2.0**100
NT = (((1,), (1,)), ((), ()))
VMEM = pl.BlockSpec(memory_space=pltpu.VMEM)
ANY = pl.BlockSpec(memory_space=pl.ANY)
SMEM = pl.BlockSpec(memory_space=pltpu.SMEM)


def head_index():
    return lax.axis_index("y") * 8 + patch_index() - IDLE


def head_slot(x, h):
    return x * SLOTS + IDLE + h


def patch_index():
    return lax.axis_index("xh") * 4 + lax.axis_index("z")


def normed(ref, rows, factor, gain, h):
    wide = ref[0, rows, h * D : (h + 1) * D].astype(jnp.float32)
    return (wide * factor * gain[h : h + 1, :]).astype(jnp.bfloat16)


def norm_factor(block):
    wide = block.astype(jnp.float32)
    return lax.rsqrt(jnp.mean(wide * wide, axis=-1, keepdims=True) + EPS)


def pack_kernel(fin_ref, q_ref, k_ref, v_ref, k_peer, v_peer, q_gain, k_gain, out_ref):
    q_factor = norm_factor(q_ref[0])
    k_factor = norm_factor(k_ref[0])
    for h in range(HEADS):
        qn = normed(q_ref, slice(None), q_factor, q_gain, h)
        kn = normed(k_ref, slice(None), k_factor, k_gain, h)
        for x in range(2):
            out_ref[head_slot(x, h), 0:TOK, :] = kn
            out_ref[head_slot(x, h), TOK : 2 * TOK, :] = v_ref[0, :, h * D : (h + 1) * D]
            out_ref[head_slot(x, h), 2 * TOK : ROWS, :] = qn[x * HALF : (x + 1) * HALF]

    fin = fin_ref[0]
    core = lax.axis_index("core")
    rows = pl.ds(pl.multiple_of(core * HALF, HALF), HALF)

    def spare(k_half, v_half):
        factor = norm_factor(k_half[0, rows, :])
        for p in range(8):
            part = slice(p * PART, (p + 1) * PART)
            for i in range(3):
                h = 3 * p + i
                kn = normed(k_half, rows, factor, k_gain, h)
                vn = v_half[0, rows, h * D : (h + 1) * D]
                for half in range(2):
                    out_ref[spare_slot(i * 4 + half), part, :] = kn[half * PART : (half + 1) * PART]
                    out_ref[spare_slot(i * 4 + 2 + half), part, :] = vn[half * PART : (half + 1) * PART]

    here = fin // 2 == lax.axis_index("xl") * 4 + lax.axis_index("y")
    pl.when(jnp.logical_and(here, fin % 2 == core))(lambda: spare(k_ref, v_ref))
    pl.when(jnp.logical_and(here, fin % 2 != core))(lambda: spare(k_peer, v_peer))


def spare_slot(e):
    return e if e < IDLE else SLOTS + e - IDLE


def q_rows(ref, t):
    return ref[pl.ds(t * 8, 8), 2 * TOK : ROWS, :].reshape(Q_ROWS, D)


def span_keys(ref, u, spans=1):
    return ref[pl.ds(u * 8, spans * 8), 0:TOK, :].reshape(spans * 8 * TOK, D)


def span_values(ref, u, spans=1):
    return ref[pl.ds(u * 8, spans * 8), TOK : 2 * TOK, :].reshape(spans * 8 * TOK, D)


def first_counted(mask_ref, core, t):
    c = 2 * t + core
    counted = mask_ref[c, 0]
    for j in range(1, 2 * t + 2 if isinstance(t, int) else SPANS):
        counted = counted + mask_ref[c, j]
    return c + 1 - counted


def own_range(first, core, t):
    return jnp.right_shift(first - core + 1, 1), t + 1


def peer_range(first, core, t):
    return jnp.right_shift(first + core, 1), t + core


def list_kernel(mask_any, list_ref, mask_ref, sem):
    copy = pltpu.make_async_copy(mask_any, mask_ref, sem.at[0])
    copy.start()
    core = lax.axis_index("core")
    copy.wait()
    firsts = [first_counted(mask_ref, core, t) for t in range(8)]
    for at, bounds in ((0, own_range), (4, peer_range)):
        pairs = singles = jnp.int32(0)
        for t in range(8):
            low, high = bounds(firsts[t], core, t)
            if at == 0 and t < LATER:
                high = high - 1
            count = high - low
            list_ref[at + 2, singles] = t
            list_ref[at + 3, singles] = high - 1
            singles = singles + jnp.bitwise_and(count, 1)

            for i in range((t + 1) // 2):
                list_ref[at, pairs + i] = t
                list_ref[at + 1, pairs + i] = low + 2 * i
            pairs = pairs + jnp.right_shift(count, 1)
        for row, total in ((at, pairs), (at + 2, singles)):
            list_ref[row, total] = 8
            list_ref[row + 1, total] = 0
            list_ref[row, 63] = total


def add_block(q, kv_ref, u, spans, row, acc_ref, tot_ref):
    scores = lax.dot_general(q, span_keys(kv_ref, u, spans), NT, preferred_element_type=jnp.float32)
    weight = jnp.exp2(scores * SCALE_LOG2)
    part = weight[:, 0:D]
    for k in range(1, spans * 8 * TOK // D):
        part = part + weight[:, k * D : (k + 1) * D]
    added = jnp.dot(weight.astype(jnp.bfloat16), span_values(kv_ref, u, spans), preferred_element_type=jnp.float32)
    acc_ref[row] += added
    tot_ref[row] += part


def accumulate(list_ref, at, q_ref, kv_ref, acc_ref, tot_ref):
    for spans, line in ((2, at), (1, at + 2)):

        def step(b, carry, spans=spans, line=line):
            for i in range(BATCH):
                row = list_ref[line, b * BATCH + i]
                q = q_rows(q_ref, jnp.minimum(row, 7))
                add_block(q, kv_ref, list_ref[line + 1, b * BATCH + i], spans, row, acc_ref, tot_ref)
            return carry

        lax.fori_loop(0, (list_ref[line, 63] + BATCH - 1) // BATCH, step, 0)


def own_kernel(list_any, own_ref, acc_ref, tot_ref, list_ref, sem):
    @pl.when(head_index() >= 0)
    def _():
        copy = pltpu.make_async_copy(list_any, list_ref, sem.at[0])
        copy.start()
        acc_ref[...] = jnp.zeros_like(acc_ref)
        tot_ref[...] = jnp.zeros_like(tot_ref)
        copy.wait()
        accumulate(list_ref, 0, own_ref, own_ref, acc_ref, tot_ref)


def peer_kernel(
    mask_any, fin_ref, list_any, own_ref, peer_ref, acc_in, tot_in, out_ref, acc_ref, tot_ref, mask_ref, list_ref, sem
):
    core = lax.axis_index("core")
    xl = lax.axis_index("xl")
    head = head_index()

    def shifted_block(q, ref, u, state):
        most, total, summed = state
        scores = lax.dot_general(q, span_keys(ref, u), NT, preferred_element_type=jnp.float32) * SCALE
        newest = jnp.maximum(most, jnp.max(scores, axis=1, keepdims=True))
        weight = jnp.exp(scores - newest)
        factor = jnp.exp(most - newest)
        total = total * factor + jnp.sum(weight, axis=1, keepdims=True)
        added = jnp.dot(weight.astype(jnp.bfloat16), span_values(ref, u), preferred_element_type=jnp.float32)
        return newest, total, summed * factor + added

    def shifted_span(t, carry):
        q = q_rows(own_ref, t)
        state = (
            jnp.full((Q_ROWS, 1), -1e30, jnp.float32),
            jnp.zeros((Q_ROWS, 1), jnp.float32),
            jnp.zeros((Q_ROWS, D), jnp.float32),
        )
        first = first_counted(mask_ref, core, t)
        low, high = own_range(first, core, t)
        state = lax.fori_loop(low, high, lambda u, s: shifted_block(q, own_ref, u, s), state)
        low, high = peer_range(first, core, t)
        state = lax.fori_loop(low, high, lambda u, s: shifted_block(q, peer_ref, u, s), state)
        _, total, summed = state
        out_ref[pl.ds(t * 8, 8), 0:HALF, :] = (summed / total).astype(jnp.bfloat16).reshape(8, HALF, D)
        return carry

    @pl.when(head >= 0)
    def _():
        copy = pltpu.make_async_copy(list_any, list_ref, sem.at[1])
        copy.start()
        for t in range(LATER):
            add_block(q_rows(own_ref, t), own_ref, t, 1, t, acc_ref, tot_ref)
        copy.wait()
        accumulate(list_ref, 4, own_ref, peer_ref, acc_ref, tot_ref)
        least = jnp.full((Q_ROWS, 1), 1.0, jnp.float32)
        largest = least
        for t in range(8):
            total = jnp.sum(tot_ref[t], axis=1, keepdims=True)
            least = jnp.minimum(least, total)
            largest = jnp.maximum(largest, total)
            attn = acc_ref[t] * (1.0 / total)
            out_ref[t * 8 : (t + 1) * 8, 0:HALF, :] = attn.astype(jnp.bfloat16).reshape(8, HALF, D)
        sound = jnp.logical_and(jnp.min(least) >= LEAST, jnp.max(largest) <= LARGEST)

        @pl.when(jnp.logical_not(sound))
        def _():
            copy = pltpu.make_async_copy(mask_any, mask_ref, sem.at[0])
            copy.start()
            copy.wait()
            lax.fori_loop(0, 8, shifted_span, 0)

    @pl.when(jnp.logical_and(head < 0, xl * IDLE + head + IDLE < SPARE))
    def _():
        fin = fin_ref[0]
        for t in range(8):
            for p in range(8):
                out_ref[t * 8 + p, 0:PART, :] = own_ref[(fin // 2) * 8 + t, p * PART : (p + 1) * PART, :]


def finish_kernel(step_ref, in_ref, gate_ref, mixed_ref, k_ref, v_ref):
    gate = gate_ref[pl.ds(step_ref[0], 1), :]
    for h in range(HEADS):
        cols = slice(h * D, (h + 1) * D)
        for x in range(2):
            rows = slice(x * HALF, (x + 1) * HALF)
            attn = in_ref[head_slot(x, h), 0:HALF, :].astype(jnp.float32)
            mixed_ref[0, rows, cols] = (attn * gate[:, cols]).astype(jnp.bfloat16)
    for e in range(SPARE):
        i, half = e // 4, e % 2
        ref = k_ref if e % 4 < 2 else v_ref
        ref[half * PART : (half + 1) * PART, i * D : (i + 1) * D] = in_ref[spare_slot(e), 0:PART, :]


PARAMS = pltpu.CompilerParams(vmem_limit_bytes=32 * 1024 * 1024)


def on_device(queries, keys, values, q_gain, k_gain, gate_table, noise_step, block_mask, finished):
    bf16 = jnp.bfloat16
    f32 = jnp.float32
    swap = [(0, 1), (1, 0)]
    k_peer = lax.ppermute(keys, "core", swap)
    v_peer = lax.ppermute(values, "core", swap)
    lists = pl.pallas_call(
        list_kernel,
        out_shape=jax.ShapeDtypeStruct((8, 64), jnp.int32),
        in_specs=[ANY],
        out_specs=SMEM,
        scratch_shapes=[pltpu.SMEM((SPANS, SPANS), jnp.int32), pltpu.SemaphoreType.DMA((1,))],
        cost_estimate=pl.CostEstimate(flops=2**32, bytes_accessed=2**12, transcendentals=0),
    )(block_mask)
    k_peer, lists = lax.optimization_barrier((k_peer, lists))
    packed = pl.pallas_call(
        pack_kernel,
        out_shape=jax.ShapeDtypeStruct((CHIPS, ROWS, D), bf16),
        in_specs=[SMEM] + [VMEM] * 7,
        out_specs=VMEM,
        compiler_params=PARAMS,
    )(finished, queries, keys, values, k_peer, v_peer, q_gain.reshape(HEADS, D), k_gain.reshape(HEADS, D))
    own = lax.all_to_all(packed, PLANE, 0, 0, tiled=True)
    peer = lax.ppermute(own, "core", swap)
    sums = [jax.ShapeDtypeStruct((9, Q_ROWS, D), f32)] * 2
    acc, tot = pl.pallas_call(
        own_kernel,
        out_shape=sums,
        in_specs=[ANY, VMEM],
        out_specs=[VMEM, VMEM],
        scratch_shapes=[pltpu.SMEM((8, 64), jnp.int32), pltpu.SemaphoreType.DMA((1,))],
        compiler_params=PARAMS,
        cost_estimate=pl.CostEstimate(flops=2**31, bytes_accessed=2**22, transcendentals=2**22),
    )(lists, own)
    outs, _, _ = pl.pallas_call(
        peer_kernel,
        out_shape=[jax.ShapeDtypeStruct((CHIPS, HALF, D), bf16)] + sums,
        in_specs=[ANY, SMEM, ANY] + [VMEM] * 4,
        out_specs=[VMEM] * 3,
        scratch_shapes=[
            pltpu.SMEM((SPANS, SPANS), jnp.int32),
            pltpu.SMEM((8, 64), jnp.int32),
            pltpu.SemaphoreType.DMA((2,)),
        ],
        input_output_aliases={5: 1, 6: 2},
        compiler_params=PARAMS,
    )(block_mask, finished, lists, own, peer, acc, tot)
    back = lax.all_to_all(outs, PLANE, 0, 0, tiled=True)
    return pl.pallas_call(
        finish_kernel,
        out_shape=(
            jax.ShapeDtypeStruct((1, TOK, HD), bf16),
            jax.ShapeDtypeStruct((HALF, 3 * D), bf16),
            jax.ShapeDtypeStruct((HALF, 3 * D), bf16),
        ),
        in_specs=[SMEM, VMEM, VMEM],
        out_specs=(VMEM, VMEM, VMEM),
        compiler_params=PARAMS,
    )(noise_step, back, gate_table)


def solution(mesh):
    fine = Mesh(mesh.devices.reshape(2, 4, 2, 2, 4), ("xl", "y", "core", "xh", "z"))
    span, patch = ("xl", "y", "core"), ("xh", "z")
    rows = P(span, patch, None)
    return jax.shard_map(
        on_device,
        mesh=fine,
        in_specs=(rows, rows, rows, P(), P(), P(), P(span), P(), P()),
        out_specs=(rows, P(span, patch), P(span, patch)),
        check_vma=False,
    )
```

```python
import math

import jax
import jax.numpy as jnp
from jax import lax
from jax.experimental import pallas as pl
from jax.experimental.pallas import tpu as pltpu
from jax.sharding import Mesh
from jax.sharding import PartitionSpec as P

D = 128
HEADS = 24
HD = HEADS * D
SPANS = 16
TOK = 64
HALF = TOK // 2
CHIPS = 64
GRID = (4, 2, 4, 2)
IDLE = 16
ROWS = 2 * TOK + HALF
SPARE = 12
PART = HALF // 2
PLANE = ("y", "xh", "z", "xl")
EPS = 1e-06
SCALE = D ** (-0.5)
SCALE_LOG2 = SCALE * math.log2(math.e)
Q_ROWS = 8 * HALF
LATER = 2
BATCH = 2
LEAST, LARGEST = 2.0**-60, 2.0**100
NT = (((1,), (1,)), ((), ()))
VMEM = pl.BlockSpec(memory_space=pltpu.VMEM)
ANY = pl.BlockSpec(memory_space=pl.ANY)
SMEM = pl.BlockSpec(memory_space=pltpu.SMEM)


def has_head():
    return lax.axis_index("y") > 0


def head_slot(x, h):
    return IDLE + x * HEADS + h


def normed(ref, rows, factor, gain, h):
    wide = ref[0, rows, h * D : (h + 1) * D].astype(jnp.float32)
    return (wide * factor * gain[h : h + 1, :]).astype(jnp.bfloat16)


def norm_factor(block):
    wide = block.astype(jnp.float32)
    return lax.rsqrt(jnp.mean(wide * wide, axis=-1, keepdims=True) + EPS)


def pack_kernel(fin_ref, q_ref, k_ref, v_ref, k_peer, v_peer, q_gain, k_gain, out_ref):
    q_factor = norm_factor(q_ref[0])
    k_factor = norm_factor(k_ref[0])
    for h in range(HEADS):
        qn = normed(q_ref, slice(None), q_factor, q_gain, h)
        kn = normed(k_ref, slice(None), k_factor, k_gain, h)
        for x in range(2):
            out_ref[head_slot(x, h), 0:TOK, :] = kn
            out_ref[head_slot(x, h), TOK : 2 * TOK, :] = v_ref[0, :, h * D : (h + 1) * D]
            out_ref[head_slot(x, h), 2 * TOK : ROWS, :] = qn[x * HALF : (x + 1) * HALF]

    fin = fin_ref[0]
    core = lax.axis_index("core")
    rows = pl.ds(pl.multiple_of(core * HALF, HALF), HALF)

    def spare(k_half, v_half):
        factor = norm_factor(k_half[0, rows, :])
        for p in range(8):
            part = slice(p * PART, (p + 1) * PART)
            for i in range(3):
                h = 3 * p + i
                kn = normed(k_half, rows, factor, k_gain, h)
                vn = v_half[0, rows, h * D : (h + 1) * D]
                for half in range(2):
                    out_ref[i * 4 + half, part, :] = kn[half * PART : (half + 1) * PART]
                    out_ref[i * 4 + 2 + half, part, :] = vn[half * PART : (half + 1) * PART]

    here = fin // 2 == lax.axis_index("xl") * 4 + lax.axis_index("y")
    pl.when(jnp.logical_and(here, fin % 2 == core))(lambda: spare(k_ref, v_ref))
    pl.when(jnp.logical_and(here, fin % 2 != core))(lambda: spare(k_peer, v_peer))


def of_span(ref, t, rows):
    return ref[jnp.bitwise_and(t, 3), :, :, jnp.right_shift(t, 2), rows, :].reshape(-1, D)


def q_rows(ref, t):
    return of_span(ref, t, slice(2 * TOK, ROWS))


def span_keys(ref, u, spans=1):
    return jnp.concatenate([of_span(ref, u + i, slice(0, TOK)) for i in range(spans)], axis=0)


def span_values(ref, u, spans=1):
    return jnp.concatenate([of_span(ref, u + i, slice(TOK, 2 * TOK)) for i in range(spans)], axis=0)


def first_counted(mask_ref, core, t):
    c = 2 * t + core
    counted = mask_ref[c, 0]
    for j in range(1, 2 * t + 2 if isinstance(t, int) else SPANS):
        counted = counted + mask_ref[c, j]
    return c + 1 - counted


def own_range(first, core, t):
    return jnp.right_shift(first - core + 1, 1), t + 1


def peer_range(first, core, t):
    return jnp.right_shift(first + core, 1), t + core


def list_kernel(mask_any, list_ref, mask_ref, sem):
    copy = pltpu.make_async_copy(mask_any, mask_ref, sem.at[0])
    copy.start()
    core = lax.axis_index("core")
    copy.wait()
    firsts = [first_counted(mask_ref, core, t) for t in range(8)]
    for at, bounds in ((0, own_range), (4, peer_range)):
        pairs = singles = jnp.int32(0)
        for t in range(8):
            low, high = bounds(firsts[t], core, t)
            if at == 0 and t < LATER:
                high = high - 1
            count = high - low
            list_ref[at + 2, singles] = t
            list_ref[at + 3, singles] = high - 1
            singles = singles + jnp.bitwise_and(count, 1)

            for i in range((t + 1) // 2):
                list_ref[at, pairs + i] = t
                list_ref[at + 1, pairs + i] = low + 2 * i
            pairs = pairs + jnp.right_shift(count, 1)
        for row, total in ((at, pairs), (at + 2, singles)):
            list_ref[row, total] = 8
            list_ref[row + 1, total] = 0
            list_ref[row, 63] = total


def add_block(q, kv_ref, u, spans, row, acc_ref, tot_ref):
    scores = lax.dot_general(q, span_keys(kv_ref, u, spans), NT, preferred_element_type=jnp.float32)
    weight = jnp.exp2(scores * SCALE_LOG2)
    part = weight[:, 0:D]
    for k in range(1, spans * 8 * TOK // D):
        part = part + weight[:, k * D : (k + 1) * D]
    added = jnp.dot(weight.astype(jnp.bfloat16), span_values(kv_ref, u, spans), preferred_element_type=jnp.float32)
    acc_ref[row] += added
    tot_ref[row] += part


def accumulate(list_ref, at, q_ref, kv_ref, acc_ref, tot_ref):
    for spans, line in ((2, at), (1, at + 2)):

        def step(b, carry, spans=spans, line=line):
            for i in range(BATCH):
                row = list_ref[line, b * BATCH + i]
                q = q_rows(q_ref, jnp.minimum(row, 7))
                add_block(q, kv_ref, list_ref[line + 1, b * BATCH + i], spans, row, acc_ref, tot_ref)
            return carry

        lax.fori_loop(0, (list_ref[line, 63] + BATCH - 1) // BATCH, step, 0)


def own_kernel(list_any, own_ref, acc_ref, tot_ref, list_ref, sem):
    @pl.when(has_head())
    def _():
        copy = pltpu.make_async_copy(list_any, list_ref, sem.at[0])
        copy.start()
        acc_ref[...] = jnp.zeros_like(acc_ref)
        tot_ref[...] = jnp.zeros_like(tot_ref)
        copy.wait()
        accumulate(list_ref, 0, own_ref, own_ref, acc_ref, tot_ref)


def peer_kernel(
    mask_any, fin_ref, list_any, own_ref, peer_ref, acc_in, tot_in, out_ref, acc_ref, tot_ref, mask_ref, list_ref, sem
):
    core = lax.axis_index("core")

    def store(t, attn):
        rows = attn.astype(jnp.bfloat16).reshape(2, 4, HALF, D)
        out_ref[jnp.bitwise_and(t, 3), :, :, jnp.right_shift(t, 2), :, :] = rows

    def shifted_block(q, ref, u, state):
        most, total, summed = state
        scores = lax.dot_general(q, span_keys(ref, u), NT, preferred_element_type=jnp.float32) * SCALE
        newest = jnp.maximum(most, jnp.max(scores, axis=1, keepdims=True))
        weight = jnp.exp(scores - newest)
        factor = jnp.exp(most - newest)
        total = total * factor + jnp.sum(weight, axis=1, keepdims=True)
        added = jnp.dot(weight.astype(jnp.bfloat16), span_values(ref, u), preferred_element_type=jnp.float32)
        return newest, total, summed * factor + added

    def shifted_span(t, carry):
        q = q_rows(own_ref, t)
        state = (
            jnp.full((Q_ROWS, 1), -1e30, jnp.float32),
            jnp.zeros((Q_ROWS, 1), jnp.float32),
            jnp.zeros((Q_ROWS, D), jnp.float32),
        )
        first = first_counted(mask_ref, core, t)
        low, high = own_range(first, core, t)
        state = lax.fori_loop(low, high, lambda u, s: shifted_block(q, own_ref, u, s), state)
        low, high = peer_range(first, core, t)
        state = lax.fori_loop(low, high, lambda u, s: shifted_block(q, peer_ref, u, s), state)
        _, total, summed = state
        store(t, summed / total)
        return carry

    @pl.when(has_head())
    def _():
        copy = pltpu.make_async_copy(list_any, list_ref, sem.at[1])
        copy.start()
        for t in range(LATER):
            add_block(q_rows(own_ref, t), own_ref, t, 1, t, acc_ref, tot_ref)
        copy.wait()
        accumulate(list_ref, 4, own_ref, peer_ref, acc_ref, tot_ref)
        least = jnp.full((Q_ROWS, 1), 1.0, jnp.float32)
        largest = least
        for t in range(8):
            total = jnp.sum(tot_ref[t], axis=1, keepdims=True)
            least = jnp.minimum(least, total)
            largest = jnp.maximum(largest, total)
            attn = acc_ref[t] * (1.0 / total)
            store(t, attn)
        sound = jnp.logical_and(jnp.min(least) >= LEAST, jnp.max(largest) <= LARGEST)

        @pl.when(jnp.logical_not(sound))
        def _():
            copy = pltpu.make_async_copy(mask_any, mask_ref, sem.at[0])
            copy.start()
            copy.wait()
            lax.fori_loop(0, 8, shifted_span, 0)

    @pl.when(jnp.logical_not(has_head()))
    def _():
        fin = jnp.right_shift(fin_ref[0], 1)
        for t in range(8):
            for p in range(8):
                rows = own_ref[fin % 4, t // 4, t % 4, fin // 4, p * PART : (p + 1) * PART, :]
                out_ref[t % 4, p // 4, p % 4, t // 4, 0:PART, :] = rows


def finish_kernel(step_ref, in_ref, gate_ref, mixed_ref, k_ref, v_ref):
    gate = gate_ref[pl.ds(step_ref[0], 1), :]
    for h in range(HEADS):
        cols = slice(h * D, (h + 1) * D)
        for x in range(2):
            rows = slice(x * HALF, (x + 1) * HALF)
            attn = in_ref[head_slot(x, h), 0:HALF, :].astype(jnp.float32)
            mixed_ref[0, rows, cols] = (attn * gate[:, cols]).astype(jnp.bfloat16)
    for e in range(SPARE):
        i, half = e // 4, e % 2
        ref = k_ref if e % 4 < 2 else v_ref
        ref[half * PART : (half + 1) * PART, i * D : (i + 1) * D] = in_ref[e, 0:PART, :]


PARAMS = pltpu.CompilerParams(vmem_limit_bytes=32 * 1024 * 1024)


def on_device(queries, keys, values, q_gain, k_gain, gate_table, noise_step, block_mask, finished):
    bf16 = jnp.bfloat16
    f32 = jnp.float32
    swap = [(0, 1), (1, 0)]
    k_peer = lax.ppermute(keys, "core", swap)
    v_peer = lax.ppermute(values, "core", swap)
    lists = pl.pallas_call(
        list_kernel,
        out_shape=jax.ShapeDtypeStruct((8, 64), jnp.int32),
        in_specs=[ANY],
        out_specs=SMEM,
        scratch_shapes=[pltpu.SMEM((SPANS, SPANS), jnp.int32), pltpu.SemaphoreType.DMA((1,))],
        cost_estimate=pl.CostEstimate(flops=2**32, bytes_accessed=2**12, transcendentals=0),
    )(block_mask)
    k_peer, lists = lax.optimization_barrier((k_peer, lists))
    packed = pl.pallas_call(
        pack_kernel,
        out_shape=jax.ShapeDtypeStruct((CHIPS, ROWS, D), bf16),
        in_specs=[SMEM] + [VMEM] * 7,
        out_specs=VMEM,
        compiler_params=PARAMS,
    )(finished, queries, keys, values, k_peer, v_peer, q_gain.reshape(HEADS, D), k_gain.reshape(HEADS, D))
    own = lax.all_to_all(packed, PLANE, 0, 0, tiled=True).reshape(*GRID, ROWS, D)
    peer = lax.ppermute(own, "core", swap)
    sums = [jax.ShapeDtypeStruct((9, Q_ROWS, D), f32)] * 2
    acc, tot = pl.pallas_call(
        own_kernel,
        out_shape=sums,
        in_specs=[ANY, VMEM],
        out_specs=[VMEM, VMEM],
        scratch_shapes=[pltpu.SMEM((8, 64), jnp.int32), pltpu.SemaphoreType.DMA((1,))],
        compiler_params=PARAMS,
        cost_estimate=pl.CostEstimate(flops=2**31, bytes_accessed=2**22, transcendentals=2**22),
    )(lists, own)
    outs, _, _ = pl.pallas_call(
        peer_kernel,
        out_shape=[jax.ShapeDtypeStruct((*GRID, HALF, D), bf16)] + sums,
        in_specs=[ANY, SMEM, ANY] + [VMEM] * 4,
        out_specs=[VMEM] * 3,
        scratch_shapes=[
            pltpu.SMEM((SPANS, SPANS), jnp.int32),
            pltpu.SMEM((8, 64), jnp.int32),
            pltpu.SemaphoreType.DMA((2,)),
        ],
        input_output_aliases={5: 1, 6: 2},
        compiler_params=PARAMS,
    )(block_mask, finished, lists, own, peer, acc, tot)
    back = lax.all_to_all(outs.reshape(CHIPS, HALF, D), PLANE, 0, 0, tiled=True)
    return pl.pallas_call(
        finish_kernel,
        out_shape=(
            jax.ShapeDtypeStruct((1, TOK, HD), bf16),
            jax.ShapeDtypeStruct((HALF, 3 * D), bf16),
            jax.ShapeDtypeStruct((HALF, 3 * D), bf16),
        ),
        in_specs=[SMEM, VMEM, VMEM],
        out_specs=(VMEM, VMEM, VMEM),
        compiler_params=PARAMS,
    )(noise_step, back, gate_table)


def solution(mesh):
    fine = Mesh(mesh.devices.reshape(2, 4, 2, 2, 4), ("xl", "y", "core", "xh", "z"))
    span, patch = ("xl", "y", "core"), ("xh", "z")
    rows = P(span, patch, None)
    return jax.shard_map(
        on_device,
        mesh=fine,
        in_specs=(rows, rows, rows, P(), P(), P(), P(span), P(), P()),
        out_specs=(rows, P(span, patch), P(span, patch)),
        check_vma=False,
    )
```

```python
import math

import jax
import jax.numpy as jnp
from jax import lax
from jax.experimental import pallas as pl
from jax.experimental.pallas import tpu as pltpu
from jax.sharding import Mesh
from jax.sharding import PartitionSpec as P

D = 128
HEADS = 24
HD = HEADS * D
SPANS = 16
TOK = 64
HALF = TOK // 2
CHIPS = 64
GRID = (4, 2, 4, 2)
IDLE = 16
ROWS = 2 * TOK + HALF
SPARE = 12
PART = HALF // 2
PLANE = ("y", "xh", "z", "xl")
EPS = 1e-06
SCALE = D ** (-0.5)
SCALE_LOG2 = SCALE * math.log2(math.e)
Q_ROWS = 8 * HALF
LATER = 2
BATCH = 2
LEAST, LARGEST = 2.0**-60, 2.0**100
NT = (((1,), (1,)), ((), ()))
VMEM = pl.BlockSpec(memory_space=pltpu.VMEM)
ANY = pl.BlockSpec(memory_space=pl.ANY)
SMEM = pl.BlockSpec(memory_space=pltpu.SMEM)


def has_head():
    return lax.axis_index("y") > 0


def head_slot(x, h):
    return IDLE + x * HEADS + h


def normed(ref, rows, factor, gain, h):
    wide = ref[0, rows, h * D : (h + 1) * D].astype(jnp.float32)
    return (wide * factor * gain[h : h + 1, :]).astype(jnp.bfloat16)


def norm_factor(block):
    wide = block.astype(jnp.float32)
    return lax.rsqrt(jnp.mean(wide * wide, axis=-1, keepdims=True) + EPS)


def pack_kernel(fin_ref, q_ref, k_ref, v_ref, k_peer, v_peer, q_gain, k_gain, out_ref):
    q_factor = norm_factor(q_ref[0])
    k_factor = norm_factor(k_ref[0])
    for h in range(HEADS):
        qn = normed(q_ref, slice(None), q_factor, q_gain, h)
        kn = normed(k_ref, slice(None), k_factor, k_gain, h)
        for x in range(2):
            out_ref[head_slot(x, h), 0:TOK, :] = kn
            out_ref[head_slot(x, h), TOK : 2 * TOK, :] = v_ref[0, :, h * D : (h + 1) * D]
            out_ref[head_slot(x, h), 2 * TOK : ROWS, :] = qn[x * HALF : (x + 1) * HALF]

    fin = fin_ref[0]
    core = lax.axis_index("core")
    rows = pl.ds(pl.multiple_of(core * HALF, HALF), HALF)

    def spare(k_half, v_half):
        factor = norm_factor(k_half[0, rows, :])
        for p in range(8):
            part = slice(p * PART, (p + 1) * PART)
            for i in range(3):
                h = 3 * p + i
                kn = normed(k_half, rows, factor, k_gain, h)
                vn = v_half[0, rows, h * D : (h + 1) * D]
                for half in range(2):
                    out_ref[i * 4 + half, part, :] = kn[half * PART : (half + 1) * PART]
                    out_ref[i * 4 + 2 + half, part, :] = vn[half * PART : (half + 1) * PART]

    here = fin // 2 == lax.axis_index("xl") * 4 + lax.axis_index("y")
    pl.when(jnp.logical_and(here, fin % 2 == core))(lambda: spare(k_ref, v_ref))
    pl.when(jnp.logical_and(here, fin % 2 != core))(lambda: spare(k_peer, v_peer))


def of_span(ref, t, rows):
    return ref[jnp.bitwise_and(t, 3), :, :, jnp.right_shift(t, 2), rows, :].reshape(-1, D)


def q_rows(ref, t):
    return of_span(ref, t, slice(2 * TOK, ROWS))


def span_keys(ref, u, spans=1):
    return jnp.concatenate([of_span(ref, u + i, slice(0, TOK)) for i in range(spans)], axis=0)


def span_values(ref, u, spans=1):
    return jnp.concatenate([of_span(ref, u + i, slice(TOK, 2 * TOK)) for i in range(spans)], axis=0)


def first_counted(mask_ref, core, t):
    c = 2 * t + core
    counted = mask_ref[c, 0]
    for j in range(1, 2 * t + 2 if isinstance(t, int) else SPANS):
        counted = counted + mask_ref[c, j]
    return c + 1 - counted


def own_range(first, core, t):
    return jnp.right_shift(first - core + 1, 1), t + 1


def peer_range(first, core, t):
    return jnp.right_shift(first + core, 1), t + core


def build_lists(mask_ref, list_ref):
    core = lax.axis_index("core")
    firsts = [first_counted(mask_ref, core, t) for t in range(8)]
    for at, bounds in ((0, own_range), (4, peer_range)):
        pairs = singles = jnp.int32(0)
        for t in range(8):
            low, high = bounds(firsts[t], core, t)
            if at == 0 and t < LATER:
                high = high - 1
            count = high - low
            list_ref[at + 2, singles] = t
            list_ref[at + 3, singles] = high - 1
            singles = singles + jnp.bitwise_and(count, 1)

            for i in range((t + 1) // 2):
                list_ref[at, pairs + i] = t
                list_ref[at + 1, pairs + i] = low + 2 * i
            pairs = pairs + jnp.right_shift(count, 1)
        for row, total in ((at, pairs), (at + 2, singles)):
            list_ref[row, total] = 8
            list_ref[row + 1, total] = 0
            list_ref[row, 63] = total


def add_block(q, kv_ref, u, spans, row, acc_ref, tot_ref):
    scores = lax.dot_general(q, span_keys(kv_ref, u, spans), NT, preferred_element_type=jnp.float32)
    weight = jnp.exp2(scores * SCALE_LOG2)
    part = weight[:, 0:D]
    for k in range(1, spans * 8 * TOK // D):
        part = part + weight[:, k * D : (k + 1) * D]
    added = jnp.dot(weight.astype(jnp.bfloat16), span_values(kv_ref, u, spans), preferred_element_type=jnp.float32)
    acc_ref[row] += added
    tot_ref[row] += part


def accumulate(list_ref, at, q_ref, kv_ref, acc_ref, tot_ref):
    for spans, line in ((2, at), (1, at + 2)):

        def step(b, carry, spans=spans, line=line):
            for i in range(BATCH):
                row = list_ref[line, b * BATCH + i]
                q = q_rows(q_ref, jnp.minimum(row, 7))
                add_block(q, kv_ref, list_ref[line + 1, b * BATCH + i], spans, row, acc_ref, tot_ref)
            return carry

        lax.fori_loop(0, (list_ref[line, 63] + BATCH - 1) // BATCH, step, 0)


def wait_kernel(out_ref):
    out_ref[...] = jnp.zeros_like(out_ref)


def own_kernel(mask_any, _, own_ref, acc_ref, tot_ref, list_any, mask_ref, list_ref, sem):
    @pl.when(has_head())
    def _():
        copy = pltpu.make_async_copy(mask_any, mask_ref, sem.at[0])
        copy.start()
        acc_ref[...] = jnp.zeros_like(acc_ref)
        tot_ref[...] = jnp.zeros_like(tot_ref)
        copy.wait()
        build_lists(mask_ref, list_ref)
        copy = pltpu.make_async_copy(list_ref, list_any, sem.at[1])
        copy.start()
        accumulate(list_ref, 0, own_ref, own_ref, acc_ref, tot_ref)
        copy.wait()


def peer_kernel(
    mask_any, fin_ref, list_any, own_ref, peer_ref, acc_in, tot_in, out_ref, acc_ref, tot_ref, mask_ref, list_ref, sem
):
    core = lax.axis_index("core")

    def store(t, attn):
        rows = attn.astype(jnp.bfloat16).reshape(2, 4, HALF, D)
        out_ref[jnp.bitwise_and(t, 3), :, :, jnp.right_shift(t, 2), :, :] = rows

    def shifted_block(q, ref, u, state):
        most, total, summed = state
        scores = lax.dot_general(q, span_keys(ref, u), NT, preferred_element_type=jnp.float32) * SCALE
        newest = jnp.maximum(most, jnp.max(scores, axis=1, keepdims=True))
        weight = jnp.exp(scores - newest)
        factor = jnp.exp(most - newest)
        total = total * factor + jnp.sum(weight, axis=1, keepdims=True)
        added = jnp.dot(weight.astype(jnp.bfloat16), span_values(ref, u), preferred_element_type=jnp.float32)
        return newest, total, summed * factor + added

    def shifted_span(t, carry):
        q = q_rows(own_ref, t)
        state = (
            jnp.full((Q_ROWS, 1), -1e30, jnp.float32),
            jnp.zeros((Q_ROWS, 1), jnp.float32),
            jnp.zeros((Q_ROWS, D), jnp.float32),
        )
        first = first_counted(mask_ref, core, t)
        low, high = own_range(first, core, t)
        state = lax.fori_loop(low, high, lambda u, s: shifted_block(q, own_ref, u, s), state)
        low, high = peer_range(first, core, t)
        state = lax.fori_loop(low, high, lambda u, s: shifted_block(q, peer_ref, u, s), state)
        _, total, summed = state
        store(t, summed / total)
        return carry

    @pl.when(has_head())
    def _():
        copy = pltpu.make_async_copy(list_any, list_ref, sem.at[1])
        copy.start()
        for t in range(LATER):
            add_block(q_rows(own_ref, t), own_ref, t, 1, t, acc_ref, tot_ref)
        copy.wait()
        accumulate(list_ref, 4, own_ref, peer_ref, acc_ref, tot_ref)
        least = jnp.full((Q_ROWS, 1), 1.0, jnp.float32)
        largest = least
        for t in range(8):
            total = jnp.sum(tot_ref[t], axis=1, keepdims=True)
            least = jnp.minimum(least, total)
            largest = jnp.maximum(largest, total)
            attn = acc_ref[t] * (1.0 / total)
            store(t, attn)
        sound = jnp.logical_and(jnp.min(least) >= LEAST, jnp.max(largest) <= LARGEST)

        @pl.when(jnp.logical_not(sound))
        def _():
            copy = pltpu.make_async_copy(mask_any, mask_ref, sem.at[0])
            copy.start()
            copy.wait()
            lax.fori_loop(0, 8, shifted_span, 0)

    @pl.when(jnp.logical_not(has_head()))
    def _():
        fin = jnp.right_shift(fin_ref[0], 1)
        for t in range(8):
            for p in range(8):
                rows = own_ref[fin % 4, t // 4, t % 4, fin // 4, p * PART : (p + 1) * PART, :]
                out_ref[t % 4, p // 4, p % 4, t // 4, 0:PART, :] = rows


def finish_kernel(step_ref, in_ref, gate_ref, mixed_ref, k_ref, v_ref):
    gate = gate_ref[pl.ds(step_ref[0], 1), :]
    for h in range(HEADS):
        cols = slice(h * D, (h + 1) * D)
        for x in range(2):
            rows = slice(x * HALF, (x + 1) * HALF)
            attn = in_ref[head_slot(x, h), 0:HALF, :].astype(jnp.float32)
            mixed_ref[0, rows, cols] = (attn * gate[:, cols]).astype(jnp.bfloat16)
    for e in range(SPARE):
        i, half = e // 4, e % 2
        ref = k_ref if e % 4 < 2 else v_ref
        ref[half * PART : (half + 1) * PART, i * D : (i + 1) * D] = in_ref[e, 0:PART, :]


PARAMS = pltpu.CompilerParams(vmem_limit_bytes=32 * 1024 * 1024)


def on_device(queries, keys, values, q_gain, k_gain, gate_table, noise_step, block_mask, finished):
    bf16 = jnp.bfloat16
    f32 = jnp.float32
    swap = [(0, 1), (1, 0)]
    k_peer = lax.ppermute(keys, "core", swap)
    v_peer = lax.ppermute(values, "core", swap)
    waited = pl.pallas_call(
        wait_kernel,
        out_shape=jax.ShapeDtypeStruct((8, D), jnp.int32),
        out_specs=VMEM,
        cost_estimate=pl.CostEstimate(flops=2**32, bytes_accessed=2**12, transcendentals=0),
    )()
    k_peer, waited = lax.optimization_barrier((k_peer, waited))
    packed = pl.pallas_call(
        pack_kernel,
        out_shape=jax.ShapeDtypeStruct((CHIPS, ROWS, D), bf16),
        in_specs=[SMEM] + [VMEM] * 7,
        out_specs=VMEM,
        compiler_params=PARAMS,
    )(finished, queries, keys, values, k_peer, v_peer, q_gain.reshape(HEADS, D), k_gain.reshape(HEADS, D))
    own = lax.all_to_all(packed, PLANE, 0, 0, tiled=True).reshape(*GRID, ROWS, D)
    peer = lax.ppermute(own, "core", swap)
    sums = [jax.ShapeDtypeStruct((9, Q_ROWS, D), f32)] * 2
    acc, tot, lists = pl.pallas_call(
        own_kernel,
        out_shape=sums + [jax.ShapeDtypeStruct((8, 64), jnp.int32)],
        in_specs=[ANY, ANY, VMEM],
        out_specs=[VMEM, VMEM, ANY],
        scratch_shapes=[
            pltpu.SMEM((SPANS, SPANS), jnp.int32),
            pltpu.SMEM((8, 64), jnp.int32),
            pltpu.SemaphoreType.DMA((2,)),
        ],
        compiler_params=PARAMS,
        cost_estimate=pl.CostEstimate(flops=2**31, bytes_accessed=2**22, transcendentals=2**22),
    )(block_mask, waited, own)
    outs, _, _ = pl.pallas_call(
        peer_kernel,
        out_shape=[jax.ShapeDtypeStruct((*GRID, HALF, D), bf16)] + sums,
        in_specs=[ANY, SMEM, ANY] + [VMEM] * 4,
        out_specs=[VMEM] * 3,
        scratch_shapes=[
            pltpu.SMEM((SPANS, SPANS), jnp.int32),
            pltpu.SMEM((8, 64), jnp.int32),
            pltpu.SemaphoreType.DMA((2,)),
        ],
        input_output_aliases={5: 1, 6: 2},
        compiler_params=PARAMS,
    )(block_mask, finished, lists, own, peer, acc, tot)
    back = lax.all_to_all(outs.reshape(CHIPS, HALF, D), PLANE, 0, 0, tiled=True)
    return pl.pallas_call(
        finish_kernel,
        out_shape=(
            jax.ShapeDtypeStruct((1, TOK, HD), bf16),
            jax.ShapeDtypeStruct((HALF, 3 * D), bf16),
            jax.ShapeDtypeStruct((HALF, 3 * D), bf16),
        ),
        in_specs=[SMEM, VMEM, VMEM],
        out_specs=(VMEM, VMEM, VMEM),
        compiler_params=PARAMS,
    )(noise_step, back, gate_table)


def solution(mesh):
    fine = Mesh(mesh.devices.reshape(2, 4, 2, 2, 4), ("xl", "y", "core", "xh", "z"))
    span, patch = ("xl", "y", "core"), ("xh", "z")
    rows = P(span, patch, None)
    return jax.shard_map(
        on_device,
        mesh=fine,
        in_specs=(rows, rows, rows, P(), P(), P(), P(span), P(), P()),
        out_specs=(rows, P(span, patch), P(span, patch)),
        check_vma=False,
    )
```
